32 devices in a mesh: rad: 2 (over x), chan: 16 (over z, y, core).
Axes of the slice: x: 2, y: 2, z: 4, core: 2. Of those that a mesh axis runs over, the one named last changes fastest.
Arguments:
- wave: float32 [512, 8, 4096], P('chan', 'rad'), may hold values from -9 to 9
- coupling: float32 [3, 512, 512], replicated, may hold values from -32 to 32
- channels: int32 [512, 3], replicated, may hold values from 0 to 3
Outputs:
- wave_out: float32 [512, 8, 4096], P('chan', 'rad')
The draws below stay inside these ranges and needn't reach their ends.
Inputs may be any that keep to these rules, and one draw needn't show every extreme that they name: `channels`: each column holds an angular momentum number.
All inputs are finite; a program needn't handle non-finite values.
Results may differ from the reference program's by a relative error of at most 0.0003.
Values sent between devices are 32-bit elements; how exact they have to be, the bound alone decides.
No kernel may reach another device: no remote copies, remote signals or barrier semaphores. Data moves between devices by JAX's collectives and lax.ppermute only.
A program may use at most 448 MiB of HBM per device.

```python
import jax
import jax.numpy as jnp
from jax import lax

CH = 512
R1 = 4096
STEPS = 1
ROWS = 8


def draw_wave(key, part):
    key = jax.random.fold_in(key, 11)
    key_modes = jax.random.fold_in(key, 1)
    key_rough = jax.random.fold_in(key, 2)
    place = (jnp.arange(R1) + 1).astype(jnp.float32) / R1
    weights = 1.1 * jax.random.normal(key_modes, (CH, ROWS, 5), jnp.float32)
    smooth = jnp.zeros((CH, ROWS, R1), jnp.float32)
    for order in range(5):
        profile = jnp.sin(jnp.pi * (order + 1.0) * place)
        smooth = smooth + weights[:, :, order:order + 1] * profile[None, None, :]
    smooth = jnp.clip(smooth, -5.0, 5.0)
    rough = jnp.clip(jax.random.normal(key_rough, (CH, ROWS, R1), jnp.float32), -3.0, 3.0)
    return (smooth + rough).astype(jnp.float32)


def place_ends(entries, key, low, largest):
    extent = entries.shape
    spot = [jax.random.randint(jax.random.fold_in(key, axis), (), 0, extent[axis]) for axis in range(len(extent))]
    entries = entries.at[tuple(spot)].set(low)
    longest = extent.index(max(extent))
    spot[longest] = (spot[longest] + 1) % extent[longest]
    return entries.at[tuple(spot)].set(largest)


def bell_draw(own_key, shape, scale, bound, kind=jnp.bfloat16):
    drawn = scale * jax.random.normal(own_key, shape, jnp.float32)
    return jnp.clip(drawn, min=-bound, max=bound).astype(kind)


def setup_inputs(seed: int = 0) -> dict:
    streams_of = jax.random.split(jax.random.key(seed), 4)
    wave = draw_wave(jax.random.fold_in(streams_of[3], 71), 0)
    coupling = bell_draw(streams_of[1], (3, CH, CH), 6.0, 32.0, jnp.float32)
    channels = place_ends(jax.random.randint(streams_of[2], (CH, 3), 0, 4), jax.random.fold_in(streams_of[2], 1), 0, 3).astype(jnp.int32)
    return {"wave": wave, "coupling": coupling, "channels": channels}


step_h = 0.25
step_tau = 0.02
row_start = 2.0
box_first = 8.0

def potential(lvalue, radius):
    return -2.0 / radius + lvalue * (lvalue + 1.0) / (2.0 * radius * radius)

def row_update(padded, centre, pot):
    lap = padded[:, 2:, :] + padded[:, :-2, :] - 2.0 * centre
    return centre - step_tau * (-0.5 / (step_h * step_h) * lap + pot * centre)

def radial_solve(field, pot, first_h):
    padded = jnp.pad(field, ((0, 0), (0, 0), (1, 1)))
    lap = padded[:, :, 2:] + padded[:, :, :-2] - 2.0 * field
    hfield = -0.5 / (first_h * first_h) * lap + pot[:, None, :] * field
    rhs = field - 0.5 * step_tau * hfield
    nchan = field.shape[0]
    length = field.shape[2]
    diag = 1.0 + 0.5 * step_tau * (1.0 / (first_h * first_h) + pot)
    offval = -step_tau / (4.0 * first_h * first_h)
    positions = jnp.arange(length)
    lower = jnp.broadcast_to(jnp.where(positions > 0, offval, 0.0), (nchan, length)).astype(diag.dtype)
    upper = jnp.broadcast_to(jnp.where(positions < length - 1, offval, 0.0), (nchan, length)).astype(diag.dtype)
    solved = lax.linalg.tridiagonal_solve(lower, diag, upper, jnp.transpose(rhs, (0, 2, 1)))
    return jnp.transpose(solved, (0, 2, 1))

def radial_factors(rfirst, rsecond):
    rmin = jnp.minimum(rsecond[:, None], rfirst[None, :])
    rmax = jnp.maximum(rsecond[:, None], rfirst[None, :])
    return jnp.stack([1.0 / rmax, rmin / (rmax * rmax), rmin * rmin / (rmax * rmax * rmax)])

def apply_repulsion(flat, mats, factors):
    total = factors[0] * jnp.dot(mats[0], flat, precision=lax.Precision.HIGHEST)
    total = total + factors[1] * jnp.dot(mats[1], flat, precision=lax.Precision.HIGHEST)
    total = total + factors[2] * jnp.dot(mats[2], flat, precision=lax.Precision.HIGHEST)
    return total

def taylor_repel(flat, mats, factors):
    first = apply_repulsion(flat, mats, factors)
    second = apply_repulsion(first, mats, factors)
    third = apply_repulsion(second, mats, factors)
    tau = step_tau
    return flat - tau * first + tau * tau / 2.0 * second - tau * tau * tau / 6.0 * third

def multipole_mats(coupling, channels):
    same = (channels[:, 2][:, None] == channels[None, :, 2]).astype(coupling.dtype)
    return 0.5 * (coupling + jnp.transpose(coupling, (0, 2, 1))) * same[None]

def reference(wave, coupling, channels):
    mats = multipole_mats(coupling, channels)
    first_h = box_first / R1
    lfirst = channels[:, 0].astype(jnp.float32)
    lsecond = channels[:, 1].astype(jnp.float32)
    rfirst = (jnp.arange(R1) + 1).astype(jnp.float32) * first_h
    rsecond = (jnp.arange(ROWS) + 1).astype(jnp.float32) * step_h + row_start
    pot_first = potential(lfirst[:, None], rfirst[None, :])
    pot_second = potential(lsecond[:, None], rsecond[None, :])
    factors = radial_factors(rfirst, rsecond).reshape(3, ROWS * R1)
    psi = wave
    for step in range(STEPS):
        padded = jnp.pad(psi, ((0, 0), (1, 1), (0, 0)))
        psi = row_update(padded, psi, pot_second[:, :, None])
        psi = radial_solve(psi, pot_first, first_h)
        flat = taylor_repel(psi.reshape(CH, ROWS * R1), mats, factors)
        psi = flat.reshape(CH, ROWS, R1)
    return psi
```

```python
import functools

import jax
import jax.numpy as jnp
import numpy as np
from jax import lax
from jax.experimental import pallas as pl
from jax.experimental.pallas import tpu as pltpu
from jax.sharding import PartitionSpec as P

step_h = 0.25
step_tau = 0.02
row_start = 2.0
box_first = 8.0
lvalues = 4
lanes = 128
vmem_bytes = 56 * 1024 * 1024


def solve_tables(length):
    first_h = box_first / length
    radius = (np.arange(length) + 1.0) * first_h
    off = -step_tau / (4.0 * first_h * first_h)
    tiles = length // lanes
    groups = np.zeros((5, lvalues, tiles, lanes))
    for lvalue in range(lvalues):
        pot = -2.0 / radius + lvalue * (lvalue + 1.0) / (2.0 * radius * radius)
        diag = 1.0 + 0.5 * step_tau * (1.0 / (first_h * first_h) + pot)
        before, ratio = np.zeros(length), np.zeros(length)
        last = 1.0
        for j in range(length):
            before[j] = last
            last = -off / (diag[j] + (off * last if j else 0.0))
            ratio[j] = last
        ratio = ratio.reshape(tiles, lanes)
        down = np.cumprod(before.reshape(tiles, lanes), axis=1)
        up = np.cumprod(ratio[:, ::-1], axis=1)[:, ::-1]
        groups[0, lvalue] = 1.0 / down
        groups[1, lvalue] = down * ratio / up
        groups[2, lvalue] = down[:, -1:]
        groups[3, lvalue] = up
        groups[4, lvalue] = up[:, :1]
    tables = groups.transpose(2, 0, 1, 3).reshape(tiles, 5 * lvalues, lanes)
    return tables.astype(np.float32), -off


def sum_weights():
    upper = np.triu(np.ones((lanes, lanes)))
    whole = np.ones((lanes, lanes))
    return np.stack([np.hstack([upper, whole]), np.hstack([upper.T, whole])])


def pick(rows, group, which):
    first = group * lvalues
    chosen = rows[first + lvalues - 1:first + lvalues]
    for lvalue in range(lvalues - 2, -1, -1):
        chosen = jnp.where(which == lvalue, rows[first + lvalue:first + lvalue + 1], chosen)
    return chosen


def tile_sums(scaled_ref, sums_ref, weight):
    for n in range(scaled_ref.shape[0]):
        size = min(256, scaled_ref.shape[1])
        for start in range(0, scaled_ref.shape[1], size):
            value = scaled_ref[n, start:start + size]
            total = None
            for _ in range(3):
                part = value.astype(jnp.bfloat16)
                value = value - part.astype(jnp.float32)
                term = jnp.dot(part, weight, preferred_element_type=jnp.float32)
                total = term if total is None else total + term
            sums_ref[n, start:start + size] = total


def solve_kernel(with_rim, scale, rad_ref, channels_ref, pots_ref, table_ref, weights_ref, *refs):
    refs = list(refs)
    sums_ref, scaled_ref, psi_ref = refs.pop(), refs.pop(), refs.pop()
    source_ref = refs.pop(0)
    rim_ref = refs.pop(0) if with_rim else None
    out_ref = refs.pop(0)
    nrows, tiles, nchan, _ = psi_ref.shape
    rad = rad_ref[0]
    which = channels_ref[...]
    side = step_tau / (2.0 * step_h * step_h)

    def columns_of(tile):
        return pl.ds(pl.multiple_of(tile * lanes, lanes), lanes)

    def rows_of(tile):
        return pl.ds(pl.multiple_of(tile * nchan, nchan), nchan)

    def fields_of(tile):
        columns = columns_of(tile)
        if with_rim:
            rim = side * rim_ref[:, columns]
            return [
                source_ref[0, :, columns] + jnp.where(rad == 0, 0.0, rim),
                source_ref[1, :, columns] + jnp.where(rad == 0, rim, 0.0),
            ]
        edge_ref, outer_ref = refs
        count = source_ref.shape[1]
        rows = [source_ref[:, r, columns] for r in range(count)]
        edge_ref[:, columns] = jnp.where(rad == 0, rows[-1], rows[0])
        centre = [
            (1.0 - 2.0 * side - step_tau * pots_ref[r]) * rows[r] for r in range(count)
        ]
        outer_ref[0, :, columns] = centre[0] + side * rows[1]
        outer_ref[1, :, columns] = centre[-1] + side * rows[-2]
        return [centre[r] + side * (rows[r - 1] + rows[r + 1]) for r in range(1, count - 1)]

    @pl.loop(0, tiles, unroll=4)
    def _(tile):
        fields = fields_of(tile)
        inverse = pick(table_ref[tile], 0, which)
        for n in range(nrows):
            psi_ref[n, tile] = fields[n]
            scaled_ref[n, rows_of(tile)] = fields[n] * inverse

    def forward(tile, carry):
        rows = table_ref[tile]
        both, decay = pick(rows, 1, which), pick(rows, 2, which)
        after = []
        for n in range(nrows):
            sums = sums_ref[n, rows_of(tile)]
            scaled_ref[n, rows_of(tile)] = both * (sums[:, :lanes] + carry[n])
            after.append(decay * (sums[:, lanes:] + carry[n]))
        return tuple(after)

    def backward(step, carry):
        tile = tiles - 1 - step
        rows = table_ref[tile]
        product, decay = pick(rows, 3, which), pick(rows, 4, which)
        after = []
        for n in range(nrows):
            sums = sums_ref[n, rows_of(tile)]
            solved = product * (sums[:, :lanes] + carry[n])
            psi_ref[n, tile] = scale * solved - psi_ref[n, tile]
            after.append(decay * (sums[:, lanes:] + carry[n]))
        return tuple(after)

    zero = tuple(jnp.zeros((nchan, lanes), jnp.float32) for _ in range(nrows))
    tile_sums(scaled_ref, sums_ref, weights_ref[0])
    lax.fori_loop(0, tiles, forward, zero, unroll=4)
    tile_sums(scaled_ref, sums_ref, weights_ref[1])
    lax.fori_loop(0, tiles, backward, zero, unroll=4)
    for n in range(nrows):
        for tile in range(tiles):
            if out_ref.ndim == 4:
                per = out_ref.shape[-1] // lanes
                column = (tile % per) * lanes
                out_ref[tile // per, n, :, column:column + lanes] = psi_ref[n, tile]
            else:
                out_ref[n, :, tile * lanes:(tile + 1) * lanes] = psi_ref[n, tile]


def solve_rows(count, place, which, pots, source, rim, parts):
    nchan, length = which.shape[0], source.shape[-1]
    tables, off = solve_tables(length)
    tiles, block = length // lanes, length // parts
    aligned = block % lanes == 0
    piece = (parts, count, nchan, block) if aligned else (count, nchan, length)
    outs = [jax.ShapeDtypeStruct(piece, jnp.float32)]
    operands = [place, which, pots, jnp.asarray(tables), jnp.asarray(sum_weights(), jnp.bfloat16)]
    operands.append(source)
    if rim is None:
        outs.append(jax.ShapeDtypeStruct((nchan, length), jnp.float32))
        outs.append(jax.ShapeDtypeStruct((2, nchan, length), jnp.float32))
    else:
        operands.append(rim)
    vmem = pl.BlockSpec(memory_space=pltpu.VMEM)
    results = pl.pallas_call(
        functools.partial(solve_kernel, rim is not None, 2.0 / off),
        out_shape=outs,
        in_specs=[pl.BlockSpec(memory_space=pltpu.SMEM)] + [vmem] * (len(operands) - 1),
        out_specs=[vmem] * len(outs),
        scratch_shapes=[
            pltpu.VMEM((count, tiles, nchan, lanes), jnp.float32),
            pltpu.VMEM((count, tiles * nchan, lanes), jnp.float32),
            pltpu.VMEM((count, tiles * nchan, 2 * lanes), jnp.float32),
        ],
        compiler_params=pltpu.CompilerParams(vmem_limit_bytes=vmem_bytes),
        cost_estimate=pl.CostEstimate(
            flops=200 * source.size, bytes_accessed=16 * source.size, transcendentals=0
        ),
        name="solve_rim" if rim is not None else "solve_inner",
    )(*operands)
    pieces = results[0]
    if not aligned:
        pieces = jnp.transpose(pieces.reshape(count, nchan, parts, block), (2, 0, 1, 3))
    return [pieces] + list(results[1:])


def mats_kernel(coupling_ref, column_ref, row_ref, out_ref):
    raw = coupling_ref[0]
    total = raw.shape[0]
    same = column_ref[...] == row_ref[...]
    mat = jnp.where(same, 0.5 * (raw + raw.T), 0.0)
    high = mat.astype(jnp.bfloat16)
    low = (mat - high.astype(jnp.float32)).astype(jnp.bfloat16)
    out_ref[0, :, 0:total] = high
    out_ref[0, :, total:2 * total] = high
    out_ref[0, :, 2 * total:3 * total] = low


def split_mats(coupling, channels):
    orders, total, _ = coupling.shape
    group = channels[:, 2]
    return pl.pallas_call(
        mats_kernel,
        grid=(orders,),
        out_shape=jax.ShapeDtypeStruct((orders, total, 3 * total), jnp.bfloat16),
        in_specs=[
            pl.BlockSpec((1, total, total), lambda k: (k, 0, 0)),
            pl.BlockSpec((total, 1), lambda k: (0, 0)),
            pl.BlockSpec((1, total), lambda k: (0, 0)),
        ],
        out_specs=pl.BlockSpec((1, total, 3 * total), lambda k: (k, 0, 0)),
        compiler_params=pltpu.CompilerParams(vmem_limit_bytes=vmem_bytes),
        cost_estimate=pl.CostEstimate(
            flops=4 * coupling.size, bytes_accessed=10 * coupling.size, transcendentals=0
        ),
        name="split_mats",
    )(coupling, group[:, None], group[None, :])


def repel_kernel(points_ref, mats_ref, factors_ref, out_ref, field_ref, parts_ref):
    orders, total, _ = mats_ref.shape
    groups, count, nchan, block = points_ref.shape
    chunk = min(256, total)

    def put(slot, start, value):
        high = value.astype(jnp.bfloat16)
        low = (value - high.astype(jnp.float32)).astype(jnp.bfloat16)
        size = value.shape[0]
        parts_ref[slot, start:start + size] = high
        parts_ref[slot, total + start:total + start + size] = low
        parts_ref[slot, 2 * total + start:2 * total + start + size] = high

    weights = (-step_tau, step_tau * step_tau / 2.0, -step_tau * step_tau * step_tau / 6.0)
    for n in range(count):
        for group in range(groups):
            field_ref[group * nchan:(group + 1) * nchan] = points_ref[group, n]
        for start in range(0, total, chunk):
            put(0, start, field_ref[start:start + chunk])
        for stage, weight in enumerate(weights):
            slot = stage % 2
            for start in range(0, total, chunk):
                rows = slice(start, start + chunk)
                value = None
                for k in range(orders):
                    term = factors_ref[n, k:k + 1] * jnp.dot(
                        mats_ref[k, rows], parts_ref[slot], preferred_element_type=jnp.float32
                    )
                    value = term if value is None else value + term
                if stage < 2:
                    put(1 - slot, start, value)
                field_ref[rows] += weight * value
        for group in range(groups):
            out_ref[group, n] = field_ref[group * nchan:(group + 1) * nchan]


def repel(points, mats, factors):
    groups, count, nchan, block = points.shape
    orders, total, _ = mats.shape
    vmem = pl.BlockSpec(memory_space=pltpu.VMEM)
    return pl.pallas_call(
        repel_kernel,
        out_shape=jax.ShapeDtypeStruct(points.shape, jnp.float32),
        in_specs=[vmem] * 3,
        out_specs=vmem,
        scratch_shapes=[
            pltpu.VMEM((total, block), jnp.float32),
            pltpu.VMEM((2, 3 * total, block), jnp.bfloat16),
        ],
        compiler_params=pltpu.CompilerParams(vmem_limit_bytes=vmem_bytes),
        cost_estimate=pl.CostEstimate(
            flops=3 * orders * 3 * 2 * total * points.size,
            bytes_accessed=2 * mats.size + 8 * points.size,
            transcendentals=0,
        ),
        name="repel",
    )(points, mats, factors)


def gather_kernel(places, *refs):
    out_ref = refs[-1]
    nchan, rows, length = out_ref.shape
    for row, (source, n) in enumerate(places):
        ref = refs[source]
        for tile in range(length // lanes):
            columns = slice(tile * lanes, (tile + 1) * lanes)
            if ref.ndim == 4:
                per = ref.shape[-1] // lanes
                column = (tile % per) * lanes
                values = ref[tile // per, n, :, column:column + lanes]
            else:
                values = ref[n, :, columns]
            out_ref[:, row, columns] = values


def gather_rows(pieces, places, shape):
    nchan, rows, length = shape
    operands = []
    for piece in pieces:
        parts, count, _, block = piece.shape
        if block % lanes:
            piece = jnp.transpose(piece, (1, 2, 0, 3)).reshape(count, nchan, length)
        operands.append(piece)
    vmem = pl.BlockSpec(memory_space=pltpu.VMEM)
    return pl.pallas_call(
        functools.partial(gather_kernel, places),
        out_shape=jax.ShapeDtypeStruct(shape, jnp.float32),
        in_specs=[vmem] * len(operands),
        out_specs=vmem,
        compiler_params=pltpu.CompilerParams(vmem_limit_bytes=vmem_bytes),
        cost_estimate=pl.CostEstimate(
            flops=0, bytes_accessed=8 * nchan * rows * length, transcendentals=0
        ),
        name="gather_rows",
    )(*operands)


def potential(lvalue, radius):
    return -2.0 / radius + lvalue * (lvalue + 1.0) / (2.0 * radius * radius)


def radial_factors(rfirst, rsecond):
    rmin = jnp.minimum(rsecond[:, None], rfirst[None, :])
    rmax = jnp.maximum(rsecond[:, None], rfirst[None, :])
    return jnp.stack(
        [1.0 / rmax, rmin / (rmax * rmax), rmin * rmin / (rmax * rmax * rmax)], axis=1
    )


def swap_halves(part, axis, devices):
    return lax.ppermute(part, axis, [(i, (i + devices // 2) % devices) for i in range(devices)])


def on_device(parts, rads, wave, coupling, channels):
    nchan, rows, length = wave.shape
    chan_index = lax.axis_index("chan")
    rad_index = lax.axis_index("rad")
    place = jnp.reshape(rad_index, (1,)).astype(jnp.int32)
    mine = lax.dynamic_slice_in_dim(channels, chan_index * nchan, nchan)
    which = jnp.broadcast_to(mine[:, 0:1], (nchan, lanes))
    rsecond = (rad_index * rows + jnp.arange(rows) + 1).astype(jnp.float32) * step_h + row_start
    pots = potential(mine[:, 1].astype(jnp.float32)[None, :], rsecond[:, None])
    pots = jnp.broadcast_to(pots[:, :, None], (rows, nchan, lanes))
    block = length // parts
    points = (chan_index * block + jnp.arange(block) + 1).astype(jnp.float32) * (box_first / length)
    factors = radial_factors(points, rsecond)
    mats = split_mats(coupling, channels)

    inner = tuple(range(1, rows - 1))
    outer = (0, rows - 1)
    more = -nchan % 8
    which = jnp.pad(which, ((0, more), (0, 0)))
    pots = jnp.pad(pots, ((0, 0), (0, more), (0, 0)))
    padded = jnp.pad(wave, ((0, more), (0, 0), (0, 0))) if more else wave
    first, edge, partial = solve_rows(len(inner), place, which, pots, padded, None, parts)
    rim = swap_halves(edge, "rad", rads)
    second, = solve_rows(len(outer), place, which, pots, partial, rim, parts)
    if more:
        first, second = first[:, :, :nchan], second[:, :, :nchan]

    def exchange(pieces):
        return lax.all_to_all(pieces, "chan", 0, 0, tiled=True)

    results = []
    for rows_here, pieces in ((inner, first), (outer, second)):
        chosen = jnp.stack([factors[r] for r in rows_here])
        results.append(exchange(repel(exchange(pieces), mats, chosen)))
    order = {r: (0, n) for n, r in enumerate(inner)}
    order.update({r: (1, n) for n, r in enumerate(outer)})
    places = tuple(order[r] for r in range(rows))
    return gather_rows(results, places, wave.shape)


def solution(mesh):
    in_specs = (P("chan", "rad", None), P(), P())
    out_specs = P("chan", "rad", None)
    return jax.shard_map(
        functools.partial(on_device, mesh.shape["chan"], mesh.shape["rad"]),
        mesh=mesh,
        in_specs=in_specs,
        out_specs=out_specs,
        check_vma=False,
    )
```

```python
import functools

import jax
import jax.numpy as jnp
import numpy as np
from jax import lax
from jax.experimental import pallas as pl
from jax.experimental.pallas import tpu as pltpu
from jax.sharding import PartitionSpec as P

step_h = 0.25
step_tau = 0.02
row_start = 2.0
box_first = 8.0
lvalues = 4
lanes = 128
vmem_bytes = 24 * 1024 * 1024
first_vmem_bytes = 60 * 1024 * 1024


def solve_tables(length):
    first_h = box_first / length
    radius = (np.arange(length) + 1.0) * first_h
    off = -step_tau / (4.0 * first_h * first_h)
    tiles = length // lanes
    groups = np.zeros((5, lvalues, tiles, lanes))
    for lvalue in range(lvalues):
        pot = -2.0 / radius + lvalue * (lvalue + 1.0) / (2.0 * radius * radius)
        diag = 1.0 + 0.5 * step_tau * (1.0 / (first_h * first_h) + pot)
        before, ratio = np.zeros(length), np.zeros(length)
        last = 1.0
        for j in range(length):
            before[j] = last
            last = -off / (diag[j] + (off * last if j else 0.0))
            ratio[j] = last
        ratio = ratio.reshape(tiles, lanes)
        down = np.cumprod(before.reshape(tiles, lanes), axis=1)
        up = np.cumprod(ratio[:, ::-1], axis=1)[:, ::-1]
        groups[0, lvalue] = 1.0 / down
        groups[1, lvalue] = down * ratio / up
        groups[2, lvalue] = down[:, -1:]
        groups[3, lvalue] = up
        groups[4, lvalue] = up[:, :1]
    tables = groups.transpose(2, 0, 1, 3).reshape(tiles, 5 * lvalues, lanes)
    return tables.astype(np.float32), -off


def sum_weights():
    upper = np.triu(np.ones((lanes, lanes)))
    whole = np.ones((lanes, lanes))
    return np.stack([np.hstack([upper, whole]), np.hstack([upper.T, whole])])


def pick(rows, group, which):
    first = group * lvalues
    chosen = rows[first + lvalues - 1:first + lvalues]
    for lvalue in range(lvalues - 2, -1, -1):
        chosen = jnp.where(which == lvalue, rows[first + lvalue:first + lvalue + 1], chosen)
    return chosen


def group_sums(value, weight):
    total = None
    for _ in range(3):
        part = value.astype(jnp.bfloat16)
        value = value - part.astype(jnp.float32)
        term = jnp.dot(part, weight, preferred_element_type=jnp.float32)
        total = term if total is None else total + term
    return total


def channel_numbers(channels_ref, column, first, nchan):
    place = lax.broadcasted_iota(jnp.int32, (nchan, lanes), 0)
    value = jnp.zeros((nchan, lanes), jnp.int32)
    count = min(nchan, channels_ref.shape[1])
    for n in range(count):
        index = jnp.minimum(first + n, channels_ref.shape[1] - 1)
        value = jnp.where(place == n, channels_ref[column, index], value)
    return value


def row_scale(channels_ref, first, nchan, row, rad, rows):
    number = channel_numbers(channels_ref, 1, first, nchan).astype(jnp.float32)
    radius = (rad * rows + row + 1).astype(jnp.float32) * step_h + row_start
    pot = potential(number, jnp.full((nchan, lanes), radius, jnp.float32))
    return (1.0 - step_tau / (step_h * step_h)) - step_tau * pot


def outer_kernel(chan_size, channels_ref, wave_ref, edge_ref, outer_ref):
    nchan, rows, length = wave_ref.shape
    side = step_tau / (2.0 * step_h * step_h)
    rad = lax.axis_index("rad")
    first = lax.axis_index("chan") * chan_size
    centre_first = row_scale(channels_ref, first, nchan, 0, rad, rows)
    centre_last = row_scale(channels_ref, first, nchan, rows - 1, rad, rows)
    for tile in range(length // lanes):
        columns = slice(tile * lanes, (tile + 1) * lanes)
        top, bottom = wave_ref[:, 0, columns], wave_ref[:, rows - 1, columns]
        edge_ref[:, columns] = jnp.where(rad == 0, bottom, top)
        outer_ref[0, :, columns] = centre_first * top + side * wave_ref[:, 1, columns]
        outer_ref[1, :, columns] = centre_last * bottom + side * wave_ref[:, rows - 2, columns]


def outer_rows(channels, wave, chan_size):
    nchan, rows, length = wave.shape
    vmem = pl.BlockSpec(memory_space=pltpu.VMEM)
    return pl.pallas_call(
        functools.partial(outer_kernel, chan_size),
        out_shape=[
            jax.ShapeDtypeStruct((nchan, length), jnp.float32),
            jax.ShapeDtypeStruct((2, nchan, length), jnp.float32),
        ],
        in_specs=[pl.BlockSpec(memory_space=pltpu.SMEM), vmem],
        out_specs=[vmem, vmem],
        compiler_params=pltpu.CompilerParams(vmem_limit_bytes=vmem_bytes),
        cost_estimate=pl.CostEstimate(
            flops=8 * wave.size, bytes_accessed=8 * wave.size, transcendentals=0
        ),
        name="outer_rows",
    )(channels, wave)


def solve_kernel(with_rim, chan_size, scale, channels_ref, table_ref, weights_ref, *refs):
    refs = list(refs)
    out_sems, stage_ref, psi_ref, ready_ref = refs.pop(), refs.pop(), refs.pop(), refs.pop()
    source_ref = refs.pop(0)
    rim_ref = refs.pop(0) if with_rim else None
    out_ref = refs.pop(0)
    nrows, tiles, nchan, _ = psi_ref.shape
    if not with_rim:
        rows_ref, in_sems = refs
    rad = lax.axis_index("rad")
    first = lax.axis_index("chan") * chan_size
    which = channel_numbers(channels_ref, 0, first, nchan)
    side = step_tau / (2.0 * step_h * step_h)
    groups = in_sems.shape[0] if not with_rim else out_sems.shape[0]
    group = tiles // groups

    def row_copies(step):
        columns = pl.ds(step * group * lanes, group * lanes)
        return [
            pltpu.make_async_copy(
                source_ref.at[:, r, columns], rows_ref.at[r, :, columns], in_sems.at[step, r]
            )
            for r in range(source_ref.shape[1])
        ]

    def out_copy(step):
        if out_ref.ndim == 4:
            here = pl.ds(step * (out_ref.shape[0] // groups), out_ref.shape[0] // groups)
            return pltpu.make_async_copy(ready_ref.at[here], out_ref.at[here], out_sems.at[step])
        here = pl.ds(step * group * lanes, group * lanes)
        return pltpu.make_async_copy(
            ready_ref.at[:, :, here], out_ref.at[:, :, here], out_sems.at[step]
        )

    if not with_rim:
        for step in range(groups):
            for copy in row_copies(step):
                copy.start()
        rows = source_ref.shape[1]
        scales = [row_scale(channels_ref, first, nchan, r, rad, rows) for r in range(1, rows - 1)]

    def fields_of(tile):
        columns = slice(tile * lanes, (tile + 1) * lanes)
        if with_rim:
            rim = side * rim_ref[:, columns]
            return [
                source_ref[0, :, columns] + jnp.where(rad == 0, 0.0, rim),
                source_ref[1, :, columns] + jnp.where(rad == 0, rim, 0.0),
            ]
        around = [rows_ref[r, :, columns] for r in range(rows)]
        return [
            scales[r - 1] * around[r] + side * (around[r - 1] + around[r + 1])
            for r in range(1, rows - 1)
        ]

    carry = [jnp.zeros((nchan, lanes), jnp.float32) for _ in range(nrows)]
    for start in range(0, tiles, group):
        if not with_rim:
            for copy in row_copies(start // group):
                copy.wait()
        scaled = [[] for _ in range(nrows)]
        for tile in range(start, start + group):
            fields = fields_of(tile)
            inverse = pick(table_ref[tile], 0, which)
            for n in range(nrows):
                psi_ref[n, tile] = fields[n]
                scaled[n].append(fields[n] * inverse)
        sums = [group_sums(jnp.concatenate(scaled[n], axis=0), weights_ref[0]) for n in range(nrows)]
        for tile in range(start, start + group):
            both, decay = pick(table_ref[tile], 1, which), pick(table_ref[tile], 2, which)
            here = slice((tile - start) * nchan, (tile - start + 1) * nchan)
            for n in range(nrows):
                stage_ref[n, tile * nchan:(tile + 1) * nchan] = both * (
                    sums[n][here, :lanes] + carry[n]
                )
                carry[n] = decay * (sums[n][here, lanes:] + carry[n])

    carry = [jnp.zeros((nchan, lanes), jnp.float32) for _ in range(nrows)]
    for start in range(tiles - group, -1, -group):
        rows_here = slice(start * nchan, (start + group) * nchan)
        sums = [group_sums(stage_ref[n, rows_here], weights_ref[1]) for n in range(nrows)]
        for tile in range(start + group - 1, start - 1, -1):
            product, decay = pick(table_ref[tile], 3, which), pick(table_ref[tile], 4, which)
            here = slice((tile - start) * nchan, (tile - start + 1) * nchan)
            for n in range(nrows):
                solved = product * (sums[n][here, :lanes] + carry[n])
                value = scale * solved - psi_ref[n, tile]
                if ready_ref.ndim == 4:
                    per = ready_ref.shape[-1] // lanes
                    column = (tile % per) * lanes
                    ready_ref[tile // per, n, :, column:column + lanes] = value
                else:
                    ready_ref[n, :, tile * lanes:(tile + 1) * lanes] = value
                carry[n] = decay * (sums[n][here, lanes:] + carry[n])
        out_copy(start // group).start()
    for step in range(groups):
        out_copy(step).wait()


def solve_rows(count, channels, source, rim, parts, chan_size):
    nchan, length = source.shape[0] if rim is None else source.shape[1], source.shape[-1]
    tables, off = solve_tables(length)
    tiles, block = length // lanes, length // parts
    aligned = block % lanes == 0
    piece = (parts, count, nchan, block) if aligned else (count, nchan, length)
    operands = [channels, jnp.asarray(tables), jnp.asarray(sum_weights(), jnp.bfloat16), source]
    if rim is not None:
        operands.append(rim)
    vmem = pl.BlockSpec(memory_space=pltpu.VMEM)
    anywhere = pl.BlockSpec(memory_space=pl.ANY)
    groups = 4
    scratch = [
        pltpu.VMEM(piece, jnp.float32),
        pltpu.VMEM((count, tiles, nchan, lanes), jnp.float32),
        pltpu.VMEM((count, tiles * nchan, lanes), jnp.float32),
        pltpu.SemaphoreType.DMA((groups,)),
    ]
    if rim is None:
        rows = source.shape[1]
        scratch = [
            pltpu.VMEM((rows, nchan, length), jnp.float32),
            pltpu.SemaphoreType.DMA((groups, rows)),
        ] + scratch
    pieces = pl.pallas_call(
        functools.partial(solve_kernel, rim is not None, chan_size, 2.0 / off),
        out_shape=jax.ShapeDtypeStruct(piece, jnp.float32),
        in_specs=[pl.BlockSpec(memory_space=pltpu.SMEM), vmem, vmem]
        + ([anywhere] if rim is None else [vmem, vmem]),
        out_specs=anywhere,
        scratch_shapes=scratch,
        compiler_params=pltpu.CompilerParams(
            vmem_limit_bytes=first_vmem_bytes if rim is None else vmem_bytes
        ),
        cost_estimate=pl.CostEstimate(
            flops=200 * source.size, bytes_accessed=16 * source.size, transcendentals=0
        ),
        name="solve_rim" if rim is not None else "solve_inner",
    )(*operands)
    if not aligned:
        pieces = jnp.transpose(pieces.reshape(count, nchan, parts, block), (2, 0, 1, 3))
    return pieces


def mats_kernel(coupling_ref, column_ref, row_ref, out_ref):
    raw = coupling_ref[0]
    total = raw.shape[0]
    same = column_ref[...] == row_ref[...]
    mat = jnp.where(same, 0.5 * (raw + raw.T), 0.0)
    high = mat.astype(jnp.bfloat16)
    low = (mat - high.astype(jnp.float32)).astype(jnp.bfloat16)
    out_ref[0, :, 0:total] = high
    out_ref[0, :, total:2 * total] = high
    out_ref[0, :, 2 * total:3 * total] = low


def split_mats(coupling, channels):
    orders, total, _ = coupling.shape
    group = channels[:, 2]
    return pl.pallas_call(
        mats_kernel,
        grid=(orders,),
        out_shape=jax.ShapeDtypeStruct((orders, total, 3 * total), jnp.bfloat16),
        in_specs=[
            pl.BlockSpec((1, total, total), lambda k: (k, 0, 0)),
            pl.BlockSpec((total, 1), lambda k: (0, 0)),
            pl.BlockSpec((1, total), lambda k: (0, 0)),
        ],
        out_specs=pl.BlockSpec((1, total, 3 * total), lambda k: (k, 0, 0)),
        compiler_params=pltpu.CompilerParams(vmem_limit_bytes=vmem_bytes),
        cost_estimate=pl.CostEstimate(
            flops=4 * coupling.size, bytes_accessed=10 * coupling.size, transcendentals=0
        ),
        name="split_mats",
    )(coupling, group[:, None], group[None, :])


def repel_kernel(points_ref, mats_ref, factors_ref, out_ref, field_ref, parts_ref):
    orders, total, _ = mats_ref.shape
    groups, count, nchan, block = points_ref.shape
    chunk = min(256, total)

    def put(slot, start, value):
        high = value.astype(jnp.bfloat16)
        low = (value - high.astype(jnp.float32)).astype(jnp.bfloat16)
        size = value.shape[0]
        parts_ref[slot, start:start + size] = high
        parts_ref[slot, total + start:total + start + size] = low
        parts_ref[slot, 2 * total + start:2 * total + start + size] = high

    weights = (-step_tau, step_tau * step_tau / 2.0, -step_tau * step_tau * step_tau / 6.0)
    for n in range(count):
        for group in range(groups):
            field_ref[group * nchan:(group + 1) * nchan] = points_ref[group, n]
        for start in range(0, total, chunk):
            put(0, start, field_ref[start:start + chunk])
        for stage, weight in enumerate(weights):
            slot = stage % 2
            for start in range(0, total, chunk):
                rows = slice(start, start + chunk)
                value = None
                for k in range(orders):
                    term = factors_ref[n, k:k + 1] * jnp.dot(
                        mats_ref[k, rows], parts_ref[slot], preferred_element_type=jnp.float32
                    )
                    value = term if value is None else value + term
                if stage < 2:
                    put(1 - slot, start, value)
                field_ref[rows] += weight * value
        for group in range(groups):
            out_ref[group, n] = field_ref[group * nchan:(group + 1) * nchan]


def repel(points, mats, factors):
    groups, count, nchan, block = points.shape
    orders, total, _ = mats.shape
    vmem = pl.BlockSpec(memory_space=pltpu.VMEM)
    return pl.pallas_call(
        repel_kernel,
        out_shape=jax.ShapeDtypeStruct(points.shape, jnp.float32),
        in_specs=[vmem] * 3,
        out_specs=vmem,
        scratch_shapes=[
            pltpu.VMEM((total, block), jnp.float32),
            pltpu.VMEM((2, 3 * total, block), jnp.bfloat16),
        ],
        compiler_params=pltpu.CompilerParams(vmem_limit_bytes=vmem_bytes),
        cost_estimate=pl.CostEstimate(
            flops=3 * orders * 3 * 2 * total * points.size,
            bytes_accessed=2 * mats.size + 8 * points.size,
            transcendentals=0,
        ),
        name="repel",
    )(points, mats, factors)


def gather_kernel(targets, piece_ref, *refs):
    sems = refs[-1]
    out_ref = refs[-2]
    length = out_ref.shape[-1]
    copies = []
    for n, row in enumerate(targets):
        if piece_ref.ndim == 4:
            parts, _, _, block = piece_ref.shape
            for part in range(parts):
                columns = pl.ds(part * block, block)
                copies.append((piece_ref.at[part, n], out_ref.at[:, row, columns]))
        else:
            copies.append((piece_ref.at[n], out_ref.at[:, row, :]))
    copies = [pltpu.make_async_copy(*ends, sems.at[k]) for k, ends in enumerate(copies)]
    for copy in copies:
        copy.start()
    for copy in copies:
        copy.wait()


def gather_rows(piece, targets, earlier, shape):
    nchan, rows, length = shape
    parts, count, _, block = piece.shape
    if block % lanes or nchan % 8:
        piece = jnp.transpose(piece, (1, 2, 0, 3)).reshape(count, nchan, length)
    anywhere = pl.BlockSpec(memory_space=pl.ANY)
    operands = [piece] if earlier is None else [piece, earlier]
    return pl.pallas_call(
        functools.partial(gather_kernel, targets),
        out_shape=jax.ShapeDtypeStruct(shape, jnp.float32),
        in_specs=[anywhere] * len(operands),
        out_specs=anywhere,
        scratch_shapes=[pltpu.SemaphoreType.DMA((count * parts,))],
        input_output_aliases={} if earlier is None else {1: 0},
        compiler_params=pltpu.CompilerParams(vmem_limit_bytes=vmem_bytes),
        cost_estimate=pl.CostEstimate(
            flops=0, bytes_accessed=4 * count * nchan * length, transcendentals=0
        ),
        name="gather_first" if earlier is None else "gather_last",
    )(*operands)


def potential(lvalue, radius):
    return -2.0 / radius + lvalue * (lvalue + 1.0) / (2.0 * radius * radius)


def radial_factors(rfirst, rsecond):
    rmin = jnp.minimum(rsecond[:, None], rfirst[None, :])
    rmax = jnp.maximum(rsecond[:, None], rfirst[None, :])
    return jnp.stack(
        [1.0 / rmax, rmin / (rmax * rmax), rmin * rmin / (rmax * rmax * rmax)], axis=1
    )


def swap_halves(part, axis, devices):
    return lax.ppermute(part, axis, [(i, (i + devices // 2) % devices) for i in range(devices)])


def on_device(parts, rads, wave, coupling, channels):
    nchan, rows, length = wave.shape
    rad_index, chan_index = lax.axis_index("rad"), lax.axis_index("chan")
    numbers = channels.T
    inner = tuple(range(1, rows - 1))
    outer = (0, rows - 1)
    more = -nchan % 8
    padded = jnp.pad(wave, ((0, more), (0, 0), (0, 0))) if more else wave

    def exchange(pieces):
        return lax.all_to_all(pieces, "chan", 0, 0, tiled=True)

    first = solve_rows(len(inner), numbers, padded, None, parts, nchan)
    edge, partial = outer_rows(numbers, padded, nchan)
    rim = swap_halves(edge, "rad", rads)
    second = solve_rows(len(outer), numbers, partial, rim, parts, nchan)
    if more:
        first, second = first[:, :, :nchan], second[:, :, :nchan]

    block = length // parts
    rsecond = (rad_index * rows + jnp.arange(rows) + 1).astype(jnp.float32) * step_h + row_start
    points = (chan_index * block + jnp.arange(block) + 1).astype(jnp.float32) * (box_first / length)
    factors = radial_factors(points, rsecond)
    mats = split_mats(coupling, channels)
    result = None
    for here, pieces in ((inner, first), (outer, second)):
        chosen = jnp.stack([factors[r] for r in here])
        pieces = exchange(repel(exchange(pieces), mats, chosen))
        result = gather_rows(pieces, here, result, wave.shape)
    return result


def solution(mesh):
    in_specs = (P("chan", "rad", None), P(), P())
    out_specs = P("chan", "rad", None)
    return jax.shard_map(
        functools.partial(on_device, mesh.shape["chan"], mesh.shape["rad"]),
        mesh=mesh,
        in_specs=in_specs,
        out_specs=out_specs,
        check_vma=False,
    )
```

```python
import functools

import jax
import jax.numpy as jnp
import numpy as np
from jax import lax
from jax.experimental import pallas as pl
from jax.experimental.pallas import tpu as pltpu
from jax.sharding import PartitionSpec as P

step_h = 0.25
step_tau = 0.02
row_start = 2.0
box_first = 8.0
lvalues = 4
lanes = 128
vmem_bytes = 24 * 1024 * 1024
first_vmem_bytes = 60 * 1024 * 1024


def solve_tables(length):
    first_h = box_first / length
    radius = (np.arange(length) + 1.0) * first_h
    off = -step_tau / (4.0 * first_h * first_h)
    tiles = length // lanes
    groups = np.zeros((5, lvalues, tiles, lanes))
    for lvalue in range(lvalues):
        pot = -2.0 / radius + lvalue * (lvalue + 1.0) / (2.0 * radius * radius)
        diag = 1.0 + 0.5 * step_tau * (1.0 / (first_h * first_h) + pot)
        before, ratio = np.zeros(length), np.zeros(length)
        last = 1.0
        for j in range(length):
            before[j] = last
            last = -off / (diag[j] + (off * last if j else 0.0))
            ratio[j] = last
        ratio = ratio.reshape(tiles, lanes)
        down = np.cumprod(before.reshape(tiles, lanes), axis=1)
        up = np.cumprod(ratio[:, ::-1], axis=1)[:, ::-1]
        groups[0, lvalue] = 1.0 / down
        groups[1, lvalue] = down * ratio / up
        groups[2, lvalue] = down[:, -1:]
        groups[3, lvalue] = up
        groups[4, lvalue] = up[:, :1]
    tables = groups.transpose(2, 0, 1, 3).reshape(tiles, 5 * lvalues, lanes)
    return tables.astype(np.float32), -off


def sum_weights():
    upper = np.triu(np.ones((lanes, lanes)))
    whole = np.ones((lanes, lanes))
    return np.stack([np.hstack([upper, whole]), np.hstack([upper.T, whole])])


def pick(rows, group, which):
    first = group * lvalues
    chosen = rows[first + lvalues - 1:first + lvalues]
    for lvalue in range(lvalues - 2, -1, -1):
        chosen = jnp.where(which == lvalue, rows[first + lvalue:first + lvalue + 1], chosen)
    return chosen


def group_sums(value, weight):
    total = None
    for _ in range(2):
        part = value.astype(jnp.bfloat16)
        value = value - part.astype(jnp.float32)
        term = jnp.dot(part, weight, preferred_element_type=jnp.float32)
        total = term if total is None else total + term
    return total


def channel_numbers(channels_ref, column, first, nchan):
    place = lax.broadcasted_iota(jnp.int32, (nchan, lanes), 0)
    value = jnp.zeros((nchan, lanes), jnp.int32)
    count = min(nchan, channels_ref.shape[1])
    for n in range(count):
        index = jnp.minimum(first + n, channels_ref.shape[1] - 1)
        value = jnp.where(place == n, channels_ref[column, index], value)
    return value


def row_scale(channels_ref, first, nchan, row, rad, rows):
    number = channel_numbers(channels_ref, 1, first, nchan).astype(jnp.float32)
    radius = (rad * rows + row + 1).astype(jnp.float32) * step_h + row_start
    pot = potential(number, jnp.full((nchan, lanes), radius, jnp.float32))
    return (1.0 - step_tau / (step_h * step_h)) - step_tau * pot


def outer_kernel(chan_size, channels_ref, wave_ref, edge_ref, outer_ref):
    nchan, rows, length = wave_ref.shape
    side = step_tau / (2.0 * step_h * step_h)
    rad = lax.axis_index("rad")
    first = lax.axis_index("chan") * chan_size
    centre_first = row_scale(channels_ref, first, nchan, 0, rad, rows)
    centre_last = row_scale(channels_ref, first, nchan, rows - 1, rad, rows)
    for tile in range(length // lanes):
        columns = slice(tile * lanes, (tile + 1) * lanes)
        top, bottom = wave_ref[:, 0, columns], wave_ref[:, rows - 1, columns]
        edge_ref[:, columns] = jnp.where(rad == 0, bottom, top)
        outer_ref[0, :, columns] = centre_first * top + side * wave_ref[:, 1, columns]
        outer_ref[1, :, columns] = centre_last * bottom + side * wave_ref[:, rows - 2, columns]


def outer_rows(channels, wave, chan_size):
    nchan, rows, length = wave.shape
    vmem = pl.BlockSpec(memory_space=pltpu.VMEM)
    return pl.pallas_call(
        functools.partial(outer_kernel, chan_size),
        out_shape=[
            jax.ShapeDtypeStruct((nchan, length), jnp.float32),
            jax.ShapeDtypeStruct((2, nchan, length), jnp.float32),
        ],
        in_specs=[pl.BlockSpec(memory_space=pltpu.SMEM), vmem],
        out_specs=[vmem, vmem],
        compiler_params=pltpu.CompilerParams(vmem_limit_bytes=vmem_bytes),
        cost_estimate=pl.CostEstimate(
            flops=8 * wave.size, bytes_accessed=8 * wave.size, transcendentals=0
        ),
        name="outer_rows",
    )(channels, wave)


def solve_kernel(with_rim, chan_size, scale, channels_ref, table_ref, weights_ref, *refs):
    refs = list(refs)
    out_sems, stage_ref, psi_ref, ready_ref = refs.pop(), refs.pop(), refs.pop(), refs.pop()
    source_ref = refs.pop(0)
    rim_ref = refs.pop(0) if with_rim else None
    out_ref = refs.pop(0)
    nrows, tiles, nchan, _ = psi_ref.shape
    if not with_rim:
        rows_ref, in_sems = refs
    rad = lax.axis_index("rad")
    first = lax.axis_index("chan") * chan_size
    which = channel_numbers(channels_ref, 0, first, nchan)
    side = step_tau / (2.0 * step_h * step_h)
    groups = in_sems.shape[0] if not with_rim else out_sems.shape[0]
    group = tiles // groups

    def row_copies(step):
        columns = pl.ds(step * group * lanes, group * lanes)
        return [
            pltpu.make_async_copy(
                source_ref.at[:, r, columns], rows_ref.at[r, :, columns], in_sems.at[step, r]
            )
            for r in range(source_ref.shape[1])
        ]

    def out_copy(step):
        if out_ref.ndim == 4:
            here = pl.ds(step * (out_ref.shape[0] // groups), out_ref.shape[0] // groups)
            return pltpu.make_async_copy(ready_ref.at[here], out_ref.at[here], out_sems.at[step])
        here = pl.ds(step * group * lanes, group * lanes)
        return pltpu.make_async_copy(
            ready_ref.at[:, :, here], out_ref.at[:, :, here], out_sems.at[step]
        )

    if not with_rim:
        for step in range(groups):
            for copy in row_copies(step):
                copy.start()
        rows = source_ref.shape[1]
        scales = [row_scale(channels_ref, first, nchan, r, rad, rows) for r in range(1, rows - 1)]

    def fields_of(tile):
        columns = slice(tile * lanes, (tile + 1) * lanes)
        if with_rim:
            rim = side * rim_ref[:, columns]
            return [
                source_ref[0, :, columns] + jnp.where(rad == 0, 0.0, rim),
                source_ref[1, :, columns] + jnp.where(rad == 0, rim, 0.0),
            ]
        around = [rows_ref[r, :, columns] for r in range(rows)]
        return [
            scales[r - 1] * around[r] + side * (around[r - 1] + around[r + 1])
            for r in range(1, rows - 1)
        ]

    carry = [jnp.zeros((nchan, lanes), jnp.float32) for _ in range(nrows)]
    for start in range(0, tiles, group):
        if not with_rim:
            for copy in row_copies(start // group):
                copy.wait()
        scaled = [[] for _ in range(nrows)]
        for tile in range(start, start + group):
            fields = fields_of(tile)
            inverse = pick(table_ref[tile], 0, which)
            for n in range(nrows):
                psi_ref[n, tile] = fields[n]
                scaled[n].append(fields[n] * inverse)
        sums = [group_sums(jnp.concatenate(scaled[n], axis=0), weights_ref[0]) for n in range(nrows)]
        for tile in range(start, start + group):
            both, decay = pick(table_ref[tile], 1, which), pick(table_ref[tile], 2, which)
            here = slice((tile - start) * nchan, (tile - start + 1) * nchan)
            for n in range(nrows):
                stage_ref[n, tile * nchan:(tile + 1) * nchan] = both * (
                    sums[n][here, :lanes] + carry[n]
                )
                carry[n] = decay * (sums[n][here, lanes:] + carry[n])

    carry = [jnp.zeros((nchan, lanes), jnp.float32) for _ in range(nrows)]
    for start in range(tiles - group, -1, -group):
        rows_here = slice(start * nchan, (start + group) * nchan)
        sums = [group_sums(stage_ref[n, rows_here], weights_ref[1]) for n in range(nrows)]
        for tile in range(start + group - 1, start - 1, -1):
            product, decay = pick(table_ref[tile], 3, which), pick(table_ref[tile], 4, which)
            here = slice((tile - start) * nchan, (tile - start + 1) * nchan)
            for n in range(nrows):
                solved = product * (sums[n][here, :lanes] + carry[n])
                value = scale * solved - psi_ref[n, tile]
                if ready_ref.ndim == 4:
                    per = ready_ref.shape[-1] // lanes
                    column = (tile % per) * lanes
                    ready_ref[tile // per, n, :, column:column + lanes] = value
                else:
                    ready_ref[n, :, tile * lanes:(tile + 1) * lanes] = value
                carry[n] = decay * (sums[n][here, lanes:] + carry[n])
        out_copy(start // group).start()
    for step in range(groups):
        out_copy(step).wait()


def solve_rows(count, channels, source, rim, parts, chan_size):
    nchan, length = source.shape[0] if rim is None else source.shape[1], source.shape[-1]
    tables, off = solve_tables(length)
    tiles, block = length // lanes, length // parts
    aligned = block % lanes == 0
    piece = (parts, count, nchan, block) if aligned else (count, nchan, length)
    operands = [channels, jnp.asarray(tables), jnp.asarray(sum_weights(), jnp.bfloat16), source]
    if rim is not None:
        operands.append(rim)
    vmem = pl.BlockSpec(memory_space=pltpu.VMEM)
    anywhere = pl.BlockSpec(memory_space=pl.ANY)
    groups = 4
    scratch = [
        pltpu.VMEM(piece, jnp.float32),
        pltpu.VMEM((count, tiles, nchan, lanes), jnp.float32),
        pltpu.VMEM((count, tiles * nchan, lanes), jnp.float32),
        pltpu.SemaphoreType.DMA((groups,)),
    ]
    if rim is None:
        rows = source.shape[1]
        scratch = [
            pltpu.VMEM((rows, nchan, length), jnp.float32),
            pltpu.SemaphoreType.DMA((groups, rows)),
        ] + scratch
    pieces = pl.pallas_call(
        functools.partial(solve_kernel, rim is not None, chan_size, 2.0 / off),
        out_shape=jax.ShapeDtypeStruct(piece, jnp.float32),
        in_specs=[pl.BlockSpec(memory_space=pltpu.SMEM), vmem, vmem]
        + ([anywhere] if rim is None else [vmem, vmem]),
        out_specs=anywhere,
        scratch_shapes=scratch,
        compiler_params=pltpu.CompilerParams(
            vmem_limit_bytes=first_vmem_bytes if rim is None else vmem_bytes
        ),
        cost_estimate=pl.CostEstimate(
            flops=200 * source.size, bytes_accessed=16 * source.size, transcendentals=0
        ),
        name="solve_rim" if rim is not None else "solve_inner",
    )(*operands)
    if not aligned:
        pieces = jnp.transpose(pieces.reshape(count, nchan, parts, block), (2, 0, 1, 3))
    return pieces


def mats_kernel(coupling_ref, column_ref, row_ref, out_ref):
    raw = coupling_ref[0]
    total = raw.shape[0]
    same = column_ref[...] == row_ref[...]
    mat = jnp.where(same, 0.5 * (raw + raw.T), 0.0)
    high = mat.astype(jnp.bfloat16)
    low = (mat - high.astype(jnp.float32)).astype(jnp.bfloat16)
    out_ref[0, :, 0:total] = high
    out_ref[0, :, total:2 * total] = high
    out_ref[0, :, 2 * total:3 * total] = low


def split_mats(coupling, channels):
    orders, total, _ = coupling.shape
    group = channels[:, 2]
    return pl.pallas_call(
        mats_kernel,
        grid=(orders,),
        out_shape=jax.ShapeDtypeStruct((orders, total, 3 * total), jnp.bfloat16),
        in_specs=[
            pl.BlockSpec((1, total, total), lambda k: (k, 0, 0)),
            pl.BlockSpec((total, 1), lambda k: (0, 0)),
            pl.BlockSpec((1, total), lambda k: (0, 0)),
        ],
        out_specs=pl.BlockSpec((1, total, 3 * total), lambda k: (k, 0, 0)),
        compiler_params=pltpu.CompilerParams(vmem_limit_bytes=vmem_bytes),
        cost_estimate=pl.CostEstimate(
            flops=4 * coupling.size, bytes_accessed=10 * coupling.size, transcendentals=0
        ),
        name="split_mats",
    )(coupling, group[:, None], group[None, :])


def repel_kernel(points_ref, mats_ref, factors_ref, out_ref, field_ref, parts_ref):
    orders, total, _ = mats_ref.shape
    groups, count, nchan, block = points_ref.shape
    chunk = min(256, total)

    def put(slot, start, value):
        high = value.astype(jnp.bfloat16)
        low = (value - high.astype(jnp.float32)).astype(jnp.bfloat16)
        size = value.shape[0]
        parts_ref[slot, start:start + size] = high
        parts_ref[slot, total + start:total + start + size] = low
        parts_ref[slot, 2 * total + start:2 * total + start + size] = high

    weights = (-step_tau, step_tau * step_tau / 2.0, -step_tau * step_tau * step_tau / 6.0)
    for n in range(count):
        for group in range(groups):
            field_ref[group * nchan:(group + 1) * nchan] = points_ref[group, n]
        for start in range(0, total, chunk):
            put(0, start, field_ref[start:start + chunk])
        for stage, weight in enumerate(weights):
            slot = stage % 2
            for start in range(0, total, chunk):
                rows = slice(start, start + chunk)
                value = None
                for k in range(orders):
                    term = factors_ref[n, k:k + 1] * jnp.dot(
                        mats_ref[k, rows], parts_ref[slot], preferred_element_type=jnp.float32
                    )
                    value = term if value is None else value + term
                if stage < 2:
                    put(1 - slot, start, value)
                field_ref[rows] += weight * value
        for group in range(groups):
            out_ref[group, n] = field_ref[group * nchan:(group + 1) * nchan]


def repel(points, mats, factors):
    groups, count, nchan, block = points.shape
    orders, total, _ = mats.shape
    vmem = pl.BlockSpec(memory_space=pltpu.VMEM)
    return pl.pallas_call(
        repel_kernel,
        out_shape=jax.ShapeDtypeStruct(points.shape, jnp.float32),
        in_specs=[vmem] * 3,
        out_specs=vmem,
        scratch_shapes=[
            pltpu.VMEM((total, block), jnp.float32),
            pltpu.VMEM((2, 3 * total, block), jnp.bfloat16),
        ],
        compiler_params=pltpu.CompilerParams(vmem_limit_bytes=vmem_bytes),
        cost_estimate=pl.CostEstimate(
            flops=3 * orders * 3 * 2 * total * points.size,
            bytes_accessed=2 * mats.size + 8 * points.size,
            transcendentals=0,
        ),
        name="repel",
    )(points, mats, factors)


def gather_kernel(targets, piece_ref, *refs):
    sems = refs[-1]
    out_ref = refs[-2]
    length = out_ref.shape[-1]
    copies = []
    for n, row in enumerate(targets):
        if piece_ref.ndim == 4:
            parts, _, _, block = piece_ref.shape
            for part in range(parts):
                columns = pl.ds(part * block, block)
                copies.append((piece_ref.at[part, n], out_ref.at[:, row, columns]))
        else:
            copies.append((piece_ref.at[n], out_ref.at[:, row, :]))
    copies = [pltpu.make_async_copy(*ends, sems.at[k]) for k, ends in enumerate(copies)]
    for copy in copies:
        copy.start()
    for copy in copies:
        copy.wait()


def gather_rows(piece, targets, earlier, shape):
    nchan, rows, length = shape
    parts, count, _, block = piece.shape
    if block % lanes or nchan % 8:
        piece = jnp.transpose(piece, (1, 2, 0, 3)).reshape(count, nchan, length)
    anywhere = pl.BlockSpec(memory_space=pl.ANY)
    operands = [piece] if earlier is None else [piece, earlier]
    return pl.pallas_call(
        functools.partial(gather_kernel, targets),
        out_shape=jax.ShapeDtypeStruct(shape, jnp.float32),
        in_specs=[anywhere] * len(operands),
        out_specs=anywhere,
        scratch_shapes=[pltpu.SemaphoreType.DMA((count * parts,))],
        input_output_aliases={} if earlier is None else {1: 0},
        compiler_params=pltpu.CompilerParams(vmem_limit_bytes=vmem_bytes),
        cost_estimate=pl.CostEstimate(
            flops=0, bytes_accessed=4 * count * nchan * length, transcendentals=0
        ),
        name="gather_first" if earlier is None else "gather_last",
    )(*operands)


def potential(lvalue, radius):
    return -2.0 / radius + lvalue * (lvalue + 1.0) / (2.0 * radius * radius)


def radial_factors(rfirst, rsecond):
    rmin = jnp.minimum(rsecond[:, None], rfirst[None, :])
    rmax = jnp.maximum(rsecond[:, None], rfirst[None, :])
    return jnp.stack(
        [1.0 / rmax, rmin / (rmax * rmax), rmin * rmin / (rmax * rmax * rmax)], axis=1
    )


def swap_halves(part, axis, devices):
    return lax.ppermute(part, axis, [(i, (i + devices // 2) % devices) for i in range(devices)])


def on_device(parts, rads, wave, coupling, channels):
    nchan, rows, length = wave.shape
    rad_index, chan_index = lax.axis_index("rad"), lax.axis_index("chan")
    numbers = channels.T
    inner = tuple(range(1, rows - 1))
    outer = (0, rows - 1)
    more = -nchan % 8
    padded = jnp.pad(wave, ((0, more), (0, 0), (0, 0))) if more else wave

    def exchange(pieces):
        return lax.all_to_all(pieces, "chan", 0, 0, tiled=True)

    first = solve_rows(len(inner), numbers, padded, None, parts, nchan)
    edge, partial = outer_rows(numbers, padded, nchan)
    rim = swap_halves(edge, "rad", rads)
    second = solve_rows(len(outer), numbers, partial, rim, parts, nchan)
    if more:
        first, second = first[:, :, :nchan], second[:, :, :nchan]

    block = length // parts
    rsecond = (rad_index * rows + jnp.arange(rows) + 1).astype(jnp.float32) * step_h + row_start
    points = (chan_index * block + jnp.arange(block) + 1).astype(jnp.float32) * (box_first / length)
    factors = radial_factors(points, rsecond)
    mats = split_mats(coupling, channels)
    result = None
    for here, pieces in ((inner, first), (outer, second)):
        chosen = jnp.stack([factors[r] for r in here])
        pieces = exchange(repel(exchange(pieces), mats, chosen))
        result = gather_rows(pieces, here, result, wave.shape)
    return result


def solution(mesh):
    in_specs = (P("chan", "rad", None), P(), P())
    out_specs = P("chan", "rad", None)
    return jax.shard_map(
        functools.partial(on_device, mesh.shape["chan"], mesh.shape["rad"]),
        mesh=mesh,
        in_specs=in_specs,
        out_specs=out_specs,
        check_vma=False,
    )
```

```python
import functools

import jax
import jax.numpy as jnp
import numpy as np
from jax import lax
from jax.experimental import pallas as pl
from jax.experimental.pallas import tpu as pltpu
from jax.sharding import PartitionSpec as P

step_h = 0.25
step_tau = 0.02
row_start = 2.0
box_first = 8.0
lvalues = 4
lanes = 128
vmem_bytes = 24 * 1024 * 1024
first_vmem_bytes = 60 * 1024 * 1024


def solve_tables(length):
    first_h = box_first / length
    radius = (np.arange(length) + 1.0) * first_h
    off = -step_tau / (4.0 * first_h * first_h)
    tiles = length // lanes
    groups = np.zeros((5, lvalues, tiles, lanes))
    for lvalue in range(lvalues):
        pot = -2.0 / radius + lvalue * (lvalue + 1.0) / (2.0 * radius * radius)
        diag = 1.0 + 0.5 * step_tau * (1.0 / (first_h * first_h) + pot)
        before, ratio = np.zeros(length), np.zeros(length)
        last = 1.0
        for j in range(length):
            before[j] = last
            last = -off / (diag[j] + (off * last if j else 0.0))
            ratio[j] = last
        ratio = ratio.reshape(tiles, lanes)
        down = np.cumprod(before.reshape(tiles, lanes), axis=1)
        up = np.cumprod(ratio[:, ::-1], axis=1)[:, ::-1]
        groups[0, lvalue] = 1.0 / down
        groups[1, lvalue] = down * ratio / up
        groups[2, lvalue] = down[:, -1:]
        groups[3, lvalue] = up
        groups[4, lvalue] = up[:, :1]
    tables = groups.transpose(2, 0, 1, 3).reshape(tiles, 5 * lvalues, lanes)
    return tables.astype(np.float32), -off


def sum_weights():
    upper = np.triu(np.ones((lanes, lanes)))
    whole = np.ones((lanes, lanes))
    return np.stack([np.hstack([upper, whole]), np.hstack([upper.T, whole])])


def pick(rows, group, which):
    first = group * lvalues
    chosen = rows[first + lvalues - 1:first + lvalues]
    for lvalue in range(lvalues - 2, -1, -1):
        chosen = jnp.where(which == lvalue, rows[first + lvalue:first + lvalue + 1], chosen)
    return chosen


def group_sums(value, weight):
    total = None
    for _ in range(2):
        part = value.astype(jnp.bfloat16)
        value = value - part.astype(jnp.float32)
        term = jnp.dot(part, weight, preferred_element_type=jnp.float32)
        total = term if total is None else total + term
    return total


def channel_numbers(channels_ref, column, first, nchan):
    place = lax.broadcasted_iota(jnp.int32, (nchan, lanes), 0)
    value = jnp.zeros((nchan, lanes), jnp.int32)
    count = min(nchan, channels_ref.shape[1])
    for n in range(count):
        index = jnp.minimum(first + n, channels_ref.shape[1] - 1)
        value = jnp.where(place == n, channels_ref[column, index], value)
    return value


def row_scale(channels_ref, first, nchan, row, rad, rows):
    number = channel_numbers(channels_ref, 1, first, nchan).astype(jnp.float32)
    radius = (rad * rows + row + 1).astype(jnp.float32) * step_h + row_start
    pot = potential(number, jnp.full((nchan, lanes), radius, jnp.float32))
    return (1.0 - step_tau / (step_h * step_h)) - step_tau * pot


def outer_kernel(chan_size, channels_ref, wave_ref, edge_ref, outer_ref):
    nchan, rows, length = wave_ref.shape
    side = step_tau / (2.0 * step_h * step_h)
    rad = lax.axis_index("rad")
    first = lax.axis_index("chan") * chan_size
    centre_first = row_scale(channels_ref, first, nchan, 0, rad, rows)
    centre_last = row_scale(channels_ref, first, nchan, rows - 1, rad, rows)
    for tile in range(length // lanes):
        columns = slice(tile * lanes, (tile + 1) * lanes)
        top, bottom = wave_ref[:, 0, columns], wave_ref[:, rows - 1, columns]
        edge_ref[:, columns] = jnp.where(rad == 0, bottom, top)
        outer_ref[0, :, columns] = centre_first * top + side * wave_ref[:, 1, columns]
        outer_ref[1, :, columns] = centre_last * bottom + side * wave_ref[:, rows - 2, columns]


def outer_rows(channels, wave, chan_size):
    nchan, rows, length = wave.shape
    vmem = pl.BlockSpec(memory_space=pltpu.VMEM)
    return pl.pallas_call(
        functools.partial(outer_kernel, chan_size),
        out_shape=[
            jax.ShapeDtypeStruct((nchan, length), jnp.float32),
            jax.ShapeDtypeStruct((2, nchan, length), jnp.float32),
        ],
        in_specs=[pl.BlockSpec(memory_space=pltpu.SMEM), vmem],
        out_specs=[vmem, vmem],
        compiler_params=pltpu.CompilerParams(vmem_limit_bytes=vmem_bytes),
        cost_estimate=pl.CostEstimate(
            flops=8 * wave.size, bytes_accessed=8 * wave.size, transcendentals=0
        ),
        name="outer_rows",
    )(channels, wave)


def solve_kernel(with_rim, chan_size, scale, channels_ref, table_ref, weights_ref, *refs):
    refs = list(refs)
    out_sems, stage_ref, psi_ref, ready_ref = refs.pop(), refs.pop(), refs.pop(), refs.pop()
    source_ref = refs.pop(0)
    rim_ref = refs.pop(0) if with_rim else None
    out_ref = refs.pop(0)
    nrows, tiles, nchan, _ = psi_ref.shape
    if not with_rim:
        rows_ref, in_sems = refs
    rad = lax.axis_index("rad")
    first = lax.axis_index("chan") * chan_size
    side = step_tau / (2.0 * step_h * step_h)
    groups = in_sems.shape[0] if not with_rim else out_sems.shape[0]
    group = tiles // groups

    def row_copies(step):
        columns = pl.ds(step * group * lanes, group * lanes)
        return [
            pltpu.make_async_copy(
                source_ref.at[:, r, columns], rows_ref.at[r, :, columns], in_sems.at[step, r]
            )
            for r in range(source_ref.shape[1])
        ]

    def out_copy(step):
        if out_ref.ndim == 4:
            here = pl.ds(step * (out_ref.shape[0] // groups), out_ref.shape[0] // groups)
            return pltpu.make_async_copy(ready_ref.at[here], out_ref.at[here], out_sems.at[step])
        here = pl.ds(step * group * lanes, group * lanes)
        return pltpu.make_async_copy(
            ready_ref.at[:, :, here], out_ref.at[:, :, here], out_sems.at[step]
        )

    if not with_rim:
        for step in range(groups):
            for copy in row_copies(step):
                copy.start()
        rows = source_ref.shape[1]
    which = channel_numbers(channels_ref, 0, first, nchan)
    if not with_rim:
        scales = [row_scale(channels_ref, first, nchan, r, rad, rows) for r in range(1, rows - 1)]

    def fields_of(tile):
        columns = slice(tile * lanes, (tile + 1) * lanes)
        if with_rim:
            rim = side * rim_ref[:, columns]
            return [
                source_ref[0, :, columns] + jnp.where(rad == 0, 0.0, rim),
                source_ref[1, :, columns] + jnp.where(rad == 0, rim, 0.0),
            ]
        around = [rows_ref[r, :, columns] for r in range(rows)]
        return [
            scales[r - 1] * around[r] + side * (around[r - 1] + around[r + 1])
            for r in range(1, rows - 1)
        ]

    carry = [jnp.zeros((nchan, lanes), jnp.float32) for _ in range(nrows)]
    for start in range(0, tiles, group):
        if not with_rim:
            for copy in row_copies(start // group):
                copy.wait()
        scaled = [[] for _ in range(nrows)]
        for tile in range(start, start + group):
            fields = fields_of(tile)
            inverse = pick(table_ref[tile], 0, which)
            for n in range(nrows):
                psi_ref[n, tile] = fields[n]
                scaled[n].append(fields[n] * inverse)
        sums = [group_sums(jnp.concatenate(scaled[n], axis=0), weights_ref[0]) for n in range(nrows)]
        for tile in range(start, start + group):
            both, decay = pick(table_ref[tile], 1, which), pick(table_ref[tile], 2, which)
            here = slice((tile - start) * nchan, (tile - start + 1) * nchan)
            for n in range(nrows):
                stage_ref[n, tile * nchan:(tile + 1) * nchan] = both * (
                    sums[n][here, :lanes] + carry[n]
                )
                carry[n] = decay * (sums[n][here, lanes:] + carry[n])

    carry = [jnp.zeros((nchan, lanes), jnp.float32) for _ in range(nrows)]
    for start in range(tiles - group, -1, -group):
        rows_here = slice(start * nchan, (start + group) * nchan)
        sums = [group_sums(stage_ref[n, rows_here], weights_ref[1]) for n in range(nrows)]
        for tile in range(start + group - 1, start - 1, -1):
            product, decay = pick(table_ref[tile], 3, which), pick(table_ref[tile], 4, which)
            here = slice((tile - start) * nchan, (tile - start + 1) * nchan)
            for n in range(nrows):
                solved = product * (sums[n][here, :lanes] + carry[n])
                value = scale * solved - psi_ref[n, tile]
                if ready_ref.ndim == 4:
                    per = ready_ref.shape[-1] // lanes
                    column = (tile % per) * lanes
                    ready_ref[tile // per, n, :, column:column + lanes] = value
                else:
                    ready_ref[n, :, tile * lanes:(tile + 1) * lanes] = value
                carry[n] = decay * (sums[n][here, lanes:] + carry[n])
        out_copy(start // group).start()
    for step in range(groups):
        out_copy(step).wait()


def solve_rows(count, channels, source, rim, parts, chan_size):
    nchan, length = source.shape[0] if rim is None else source.shape[1], source.shape[-1]
    tables, off = solve_tables(length)
    tiles, block = length // lanes, length // parts
    aligned = block % lanes == 0
    piece = (parts, count, nchan, block) if aligned else (count, nchan, length)
    operands = [channels, jnp.asarray(tables), jnp.asarray(sum_weights(), jnp.bfloat16), source]
    if rim is not None:
        operands.append(rim)
    vmem = pl.BlockSpec(memory_space=pltpu.VMEM)
    anywhere = pl.BlockSpec(memory_space=pl.ANY)
    groups = 4
    scratch = [
        pltpu.VMEM(piece, jnp.float32),
        pltpu.VMEM((count, tiles, nchan, lanes), jnp.float32),
        pltpu.VMEM((count, tiles * nchan, lanes), jnp.float32),
        pltpu.SemaphoreType.DMA((groups,)),
    ]
    if rim is None:
        rows = source.shape[1]
        scratch = [
            pltpu.VMEM((rows, nchan, length), jnp.float32),
            pltpu.SemaphoreType.DMA((groups, rows)),
        ] + scratch
    pieces = pl.pallas_call(
        functools.partial(solve_kernel, rim is not None, chan_size, 2.0 / off),
        out_shape=jax.ShapeDtypeStruct(piece, jnp.float32),
        in_specs=[pl.BlockSpec(memory_space=pltpu.SMEM), vmem, vmem]
        + ([anywhere] if rim is None else [vmem, vmem]),
        out_specs=anywhere,
        scratch_shapes=scratch,
        compiler_params=pltpu.CompilerParams(
            vmem_limit_bytes=first_vmem_bytes if rim is None else vmem_bytes
        ),
        cost_estimate=pl.CostEstimate(
            flops=200 * source.size, bytes_accessed=16 * source.size, transcendentals=0
        ),
        name="solve_rim" if rim is not None else "solve_inner",
    )(*operands)
    if not aligned:
        pieces = jnp.transpose(pieces.reshape(count, nchan, parts, block), (2, 0, 1, 3))
    return pieces


def mats_kernel(coupling_ref, column_ref, row_ref, out_ref):
    raw = coupling_ref[0]
    total = raw.shape[0]
    same = column_ref[...] == row_ref[...]
    mat = jnp.where(same, 0.5 * (raw + raw.T), 0.0)
    high = mat.astype(jnp.bfloat16)
    low = (mat - high.astype(jnp.float32)).astype(jnp.bfloat16)
    out_ref[0, :, 0:total] = high
    out_ref[0, :, total:2 * total] = high
    out_ref[0, :, 2 * total:3 * total] = low


def split_mats(coupling, channels):
    orders, total, _ = coupling.shape
    group = channels[:, 2]
    return pl.pallas_call(
        mats_kernel,
        grid=(orders,),
        out_shape=jax.ShapeDtypeStruct((orders, total, 3 * total), jnp.bfloat16),
        in_specs=[
            pl.BlockSpec((1, total, total), lambda k: (k, 0, 0)),
            pl.BlockSpec((total, 1), lambda k: (0, 0)),
            pl.BlockSpec((1, total), lambda k: (0, 0)),
        ],
        out_specs=pl.BlockSpec((1, total, 3 * total), lambda k: (k, 0, 0)),
        compiler_params=pltpu.CompilerParams(vmem_limit_bytes=vmem_bytes),
        cost_estimate=pl.CostEstimate(
            flops=4 * coupling.size, bytes_accessed=10 * coupling.size, transcendentals=0
        ),
        name="split_mats",
    )(coupling, group[:, None], group[None, :])


def repel_kernel(points_ref, mats_ref, factors_ref, out_ref, field_ref, parts_ref):
    orders, total, _ = mats_ref.shape
    groups, count, nchan, block = points_ref.shape
    chunk = min(256, total)

    def put(slot, start, value):
        high = value.astype(jnp.bfloat16)
        low = (value - high.astype(jnp.float32)).astype(jnp.bfloat16)
        size = value.shape[0]
        parts_ref[slot, start:start + size] = high
        parts_ref[slot, total + start:total + start + size] = low
        parts_ref[slot, 2 * total + start:2 * total + start + size] = high

    weights = (-step_tau, step_tau * step_tau / 2.0, -step_tau * step_tau * step_tau / 6.0)
    for n in range(count):
        for group in range(groups):
            field_ref[group * nchan:(group + 1) * nchan] = points_ref[group, n]
        for start in range(0, total, chunk):
            put(0, start, field_ref[start:start + chunk])
        for stage, weight in enumerate(weights):
            slot = stage % 2
            for start in range(0, total, chunk):
                rows = slice(start, start + chunk)
                value = None
                for k in range(orders):
                    term = factors_ref[n, k:k + 1] * jnp.dot(
                        mats_ref[k, rows], parts_ref[slot], preferred_element_type=jnp.float32
                    )
                    value = term if value is None else value + term
                if stage < 2:
                    put(1 - slot, start, value)
                field_ref[rows] += weight * value
        for group in range(groups):
            out_ref[group, n] = field_ref[group * nchan:(group + 1) * nchan]


def repel(points, mats, factors):
    groups, count, nchan, block = points.shape
    orders, total, _ = mats.shape
    vmem = pl.BlockSpec(memory_space=pltpu.VMEM)
    return pl.pallas_call(
        repel_kernel,
        out_shape=jax.ShapeDtypeStruct(points.shape, jnp.float32),
        in_specs=[vmem] * 3,
        out_specs=vmem,
        scratch_shapes=[
            pltpu.VMEM((total, block), jnp.float32),
            pltpu.VMEM((2, 3 * total, block), jnp.bfloat16),
        ],
        compiler_params=pltpu.CompilerParams(vmem_limit_bytes=vmem_bytes),
        cost_estimate=pl.CostEstimate(
            flops=3 * orders * 3 * 2 * total * points.size,
            bytes_accessed=2 * mats.size + 8 * points.size,
            transcendentals=0,
        ),
        name="repel",
    )(points, mats, factors)


def gather_kernel(targets, piece_ref, *refs):
    sems = refs[-1]
    out_ref = refs[-2]
    length = out_ref.shape[-1]
    copies = []
    for n, row in enumerate(targets):
        if piece_ref.ndim == 4:
            parts, _, _, block = piece_ref.shape
            for part in range(parts):
                columns = pl.ds(part * block, block)
                copies.append((piece_ref.at[part, n], out_ref.at[:, row, columns]))
        else:
            copies.append((piece_ref.at[n], out_ref.at[:, row, :]))
    copies = [pltpu.make_async_copy(*ends, sems.at[k]) for k, ends in enumerate(copies)]
    for copy in copies:
        copy.start()
    for copy in copies:
        copy.wait()


def gather_rows(piece, targets, earlier, shape):
    nchan, rows, length = shape
    parts, count, _, block = piece.shape
    if block % lanes or nchan % 8:
        piece = jnp.transpose(piece, (1, 2, 0, 3)).reshape(count, nchan, length)
    anywhere = pl.BlockSpec(memory_space=pl.ANY)
    operands = [piece] if earlier is None else [piece, earlier]
    return pl.pallas_call(
        functools.partial(gather_kernel, targets),
        out_shape=jax.ShapeDtypeStruct(shape, jnp.float32),
        in_specs=[anywhere] * len(operands),
        out_specs=anywhere,
        scratch_shapes=[pltpu.SemaphoreType.DMA((count * parts,))],
        input_output_aliases={} if earlier is None else {1: 0},
        compiler_params=pltpu.CompilerParams(vmem_limit_bytes=vmem_bytes),
        cost_estimate=pl.CostEstimate(
            flops=0, bytes_accessed=4 * count * nchan * length, transcendentals=0
        ),
        name="gather_first" if earlier is None else "gather_last",
    )(*operands)


def potential(lvalue, radius):
    return -2.0 / radius + lvalue * (lvalue + 1.0) / (2.0 * radius * radius)


def radial_factors(rfirst, rsecond):
    rmin = jnp.minimum(rsecond[:, None], rfirst[None, :])
    rmax = jnp.maximum(rsecond[:, None], rfirst[None, :])
    return jnp.stack(
        [1.0 / rmax, rmin / (rmax * rmax), rmin * rmin / (rmax * rmax * rmax)], axis=1
    )


def swap_halves(part, axis, devices):
    return lax.ppermute(part, axis, [(i, (i + devices // 2) % devices) for i in range(devices)])


def on_device(parts, rads, wave, coupling, channels):
    nchan, rows, length = wave.shape
    rad_index, chan_index = lax.axis_index("rad"), lax.axis_index("chan")
    numbers = channels.T
    inner = tuple(range(1, rows - 1))
    outer = (0, rows - 1)
    more = -nchan % 8
    padded = jnp.pad(wave, ((0, more), (0, 0), (0, 0))) if more else wave

    def exchange(pieces):
        return lax.all_to_all(pieces, "chan", 0, 0, tiled=True)

    first = solve_rows(len(inner), numbers, padded, None, parts, nchan)
    edge, partial = outer_rows(numbers, padded, nchan)
    rim = swap_halves(edge, "rad", rads)
    second = solve_rows(len(outer), numbers, partial, rim, parts, nchan)
    if more:
        first, second = first[:, :, :nchan], second[:, :, :nchan]

    block = length // parts
    rsecond = (rad_index * rows + jnp.arange(rows) + 1).astype(jnp.float32) * step_h + row_start
    points = (chan_index * block + jnp.arange(block) + 1).astype(jnp.float32) * (box_first / length)
    factors = radial_factors(points, rsecond)
    mats = split_mats(coupling, channels)
    result = None
    for here, pieces in ((inner, first), (outer, second)):
        chosen = jnp.stack([factors[r] for r in here])
        pieces = exchange(repel(exchange(pieces), mats, chosen))
        result = gather_rows(pieces, here, result, wave.shape)
    return result


def solution(mesh):
    in_specs = (P("chan", "rad", None), P(), P())
    out_specs = P("chan", "rad", None)
    return jax.shard_map(
        functools.partial(on_device, mesh.shape["chan"], mesh.shape["rad"]),
        mesh=mesh,
        in_specs=in_specs,
        out_specs=out_specs,
        check_vma=False,
    )
```

```python
import functools

import jax
import jax.numpy as jnp
import numpy as np
from jax import lax
from jax.experimental import pallas as pl
from jax.experimental.pallas import tpu as pltpu
from jax.sharding import PartitionSpec as P

step_h = 0.25
step_tau = 0.02
row_start = 2.0
box_first = 8.0
lvalues = 4
lanes = 128
vmem_bytes = 24 * 1024 * 1024
first_vmem_bytes = 60 * 1024 * 1024


def solve_tables(length):
    first_h = box_first / length
    radius = (np.arange(length) + 1.0) * first_h
    off = -step_tau / (4.0 * first_h * first_h)
    tiles = length // lanes
    groups = np.zeros((5, lvalues, tiles, lanes))
    for lvalue in range(lvalues):
        pot = -2.0 / radius + lvalue * (lvalue + 1.0) / (2.0 * radius * radius)
        diag = 1.0 + 0.5 * step_tau * (1.0 / (first_h * first_h) + pot)
        before, ratio = np.zeros(length), np.zeros(length)
        last = 1.0
        for j in range(length):
            before[j] = last
            last = -off / (diag[j] + (off * last if j else 0.0))
            ratio[j] = last
        ratio = ratio.reshape(tiles, lanes)
        down = np.cumprod(before.reshape(tiles, lanes), axis=1)
        up = np.cumprod(ratio[:, ::-1], axis=1)[:, ::-1]
        groups[0, lvalue] = 1.0 / down
        groups[1, lvalue] = down * ratio / up
        groups[2, lvalue] = down[:, -1:]
        groups[3, lvalue] = up
        groups[4, lvalue] = up[:, :1]
    tables = groups.transpose(2, 0, 1, 3).reshape(tiles, 5 * lvalues, lanes)
    return tables.astype(np.float32), -off


def sum_weights():
    upper = np.triu(np.ones((lanes, lanes)))
    whole = np.ones((lanes, lanes))
    return np.stack([np.hstack([upper, whole]), np.hstack([upper.T, whole])])


def pick(rows, group, which):
    first = group * lvalues
    chosen = rows[first + lvalues - 1:first + lvalues]
    for lvalue in range(lvalues - 2, -1, -1):
        chosen = jnp.where(which == lvalue, rows[first + lvalue:first + lvalue + 1], chosen)
    return chosen


def group_sums(value, weight):
    total = None
    for _ in range(2):
        part = value.astype(jnp.bfloat16)
        value = value - part.astype(jnp.float32)
        term = jnp.dot(part, weight, preferred_element_type=jnp.float32)
        total = term if total is None else total + term
    return total


def channel_numbers(channels_ref, column, first, nchan):
    place = lax.broadcasted_iota(jnp.int32, (nchan, lanes), 0)
    value = jnp.zeros((nchan, lanes), jnp.int32)
    count = min(nchan, channels_ref.shape[1])
    for n in range(count):
        index = jnp.minimum(first + n, channels_ref.shape[1] - 1)
        value = jnp.where(place == n, channels_ref[column, index], value)
    return value


def row_scale(channels_ref, first, nchan, row, rad, rows):
    number = channel_numbers(channels_ref, 1, first, nchan).astype(jnp.float32)
    radius = (rad * rows + row + 1).astype(jnp.float32) * step_h + row_start
    pot = potential(number, jnp.full((nchan, lanes), radius, jnp.float32))
    return (1.0 - step_tau / (step_h * step_h)) - step_tau * pot


def outer_kernel(chan_size, channels_ref, wave_ref, edge_ref, outer_ref):
    nchan, rows, length = wave_ref.shape
    side = step_tau / (2.0 * step_h * step_h)
    rad = lax.axis_index("rad")
    first = lax.axis_index("chan") * chan_size
    centre_first = row_scale(channels_ref, first, nchan, 0, rad, rows)
    centre_last = row_scale(channels_ref, first, nchan, rows - 1, rad, rows)
    for tile in range(length // lanes):
        columns = slice(tile * lanes, (tile + 1) * lanes)
        top, bottom = wave_ref[:, 0, columns], wave_ref[:, rows - 1, columns]
        edge_ref[:, columns] = jnp.where(rad == 0, bottom, top)
        outer_ref[0, :, columns] = centre_first * top + side * wave_ref[:, 1, columns]
        outer_ref[1, :, columns] = centre_last * bottom + side * wave_ref[:, rows - 2, columns]


def outer_rows(channels, wave, chan_size):
    nchan, rows, length = wave.shape
    vmem = pl.BlockSpec(memory_space=pltpu.VMEM)
    return pl.pallas_call(
        functools.partial(outer_kernel, chan_size),
        out_shape=[
            jax.ShapeDtypeStruct((nchan, length), jnp.float32),
            jax.ShapeDtypeStruct((2, nchan, length), jnp.float32),
        ],
        in_specs=[pl.BlockSpec(memory_space=pltpu.SMEM), vmem],
        out_specs=[vmem, vmem],
        compiler_params=pltpu.CompilerParams(vmem_limit_bytes=vmem_bytes),
        cost_estimate=pl.CostEstimate(
            flops=8 * wave.size, bytes_accessed=8 * wave.size, transcendentals=0
        ),
        name="outer_rows",
    )(channels, wave)


def solve_kernel(with_rim, chan_size, scale, channels_ref, table_ref, weights_ref, *refs):
    refs = list(refs)
    out_sems, stage_ref, psi_ref, ready_ref = refs.pop(), refs.pop(), refs.pop(), refs.pop()
    source_ref = refs.pop(0)
    rim_ref = refs.pop(0) if with_rim else None
    out_ref = refs.pop(0)
    nrows, tiles, nchan, _ = psi_ref.shape
    if not with_rim:
        rows_ref, in_sems = refs
    rad = lax.axis_index("rad")
    first = lax.axis_index("chan") * chan_size
    which = channel_numbers(channels_ref, 0, first, nchan)
    side = step_tau / (2.0 * step_h * step_h)
    groups = in_sems.shape[0] if not with_rim else out_sems.shape[0]
    group = tiles // groups

    def row_copies(step):
        columns = pl.ds(step * group * lanes, group * lanes)
        return [
            pltpu.make_async_copy(
                source_ref.at[:, r, columns], rows_ref.at[r, :, columns], in_sems.at[step, r]
            )
            for r in range(source_ref.shape[1])
        ]

    def out_copy(step):
        if out_ref.ndim == 4:
            here = pl.ds(step * (out_ref.shape[0] // groups), out_ref.shape[0] // groups)
            return pltpu.make_async_copy(ready_ref.at[here], out_ref.at[here], out_sems.at[step])
        here = pl.ds(step * group * lanes, group * lanes)
        return pltpu.make_async_copy(
            ready_ref.at[:, :, here], out_ref.at[:, :, here], out_sems.at[step]
        )

    if not with_rim:
        for step in range(groups):
            for copy in row_copies(step):
                copy.start()
        rows = source_ref.shape[1]
        scales = [row_scale(channels_ref, first, nchan, r, rad, rows) for r in range(1, rows - 1)]

    def fields_of(tile):
        columns = slice(tile * lanes, (tile + 1) * lanes)
        if with_rim:
            rim = side * rim_ref[:, columns]
            return [
                source_ref[0, :, columns] + jnp.where(rad == 0, 0.0, rim),
                source_ref[1, :, columns] + jnp.where(rad == 0, rim, 0.0),
            ]
        around = [rows_ref[r, :, columns] for r in range(rows)]
        return [
            scales[r - 1] * around[r] + side * (around[r - 1] + around[r + 1])
            for r in range(1, rows - 1)
        ]

    carry = [jnp.zeros((nchan, lanes), jnp.float32) for _ in range(nrows)]
    for start in range(0, tiles, group):
        if not with_rim:
            for copy in row_copies(start // group):
                copy.wait()
        scaled = [[] for _ in range(nrows)]
        for tile in range(start, start + group):
            fields = fields_of(tile)
            inverse = pick(table_ref[tile], 0, which)
            for n in range(nrows):
                psi_ref[n, tile] = fields[n]
                scaled[n].append(fields[n] * inverse)
        sums = [group_sums(jnp.concatenate(scaled[n], axis=0), weights_ref[0]) for n in range(nrows)]
        for tile in range(start, start + group):
            both, decay = pick(table_ref[tile], 1, which), pick(table_ref[tile], 2, which)
            here = slice((tile - start) * nchan, (tile - start + 1) * nchan)
            for n in range(nrows):
                stage_ref[n, tile * nchan:(tile + 1) * nchan] = both * (
                    sums[n][here, :lanes] + carry[n]
                )
                carry[n] = decay * (sums[n][here, lanes:] + carry[n])

    carry = [jnp.zeros((nchan, lanes), jnp.float32) for _ in range(nrows)]
    for start in range(tiles - group, -1, -group):
        rows_here = slice(start * nchan, (start + group) * nchan)
        sums = [group_sums(stage_ref[n, rows_here], weights_ref[1]) for n in range(nrows)]
        for tile in range(start + group - 1, start - 1, -1):
            product, decay = pick(table_ref[tile], 3, which), pick(table_ref[tile], 4, which)
            here = slice((tile - start) * nchan, (tile - start + 1) * nchan)
            for n in range(nrows):
                solved = product * (sums[n][here, :lanes] + carry[n])
                value = scale * solved - psi_ref[n, tile]
                if ready_ref.ndim == 4:
                    per = ready_ref.shape[-1] // lanes
                    column = (tile % per) * lanes
                    ready_ref[tile // per, n, :, column:column + lanes] = value
                else:
                    ready_ref[n, :, tile * lanes:(tile + 1) * lanes] = value
                carry[n] = decay * (sums[n][here, lanes:] + carry[n])
        out_copy(start // group).start()
    for step in range(groups):
        out_copy(step).wait()


def solve_rows(count, channels, source, rim, parts, chan_size):
    nchan, length = source.shape[0] if rim is None else source.shape[1], source.shape[-1]
    tables, off = solve_tables(length)
    tiles, block = length // lanes, length // parts
    aligned = block % lanes == 0
    piece = (parts, count, nchan, block) if aligned else (count, nchan, length)
    operands = [channels, jnp.asarray(tables), jnp.asarray(sum_weights(), jnp.bfloat16), source]
    if rim is not None:
        operands.append(rim)
    vmem = pl.BlockSpec(memory_space=pltpu.VMEM)
    anywhere = pl.BlockSpec(memory_space=pl.ANY)
    groups = 2
    scratch = [
        pltpu.VMEM(piece, jnp.float32),
        pltpu.VMEM((count, tiles, nchan, lanes), jnp.float32),
        pltpu.VMEM((count, tiles * nchan, lanes), jnp.float32),
        pltpu.SemaphoreType.DMA((groups,)),
    ]
    if rim is None:
        rows = source.shape[1]
        scratch = [
            pltpu.VMEM((rows, nchan, length), jnp.float32),
            pltpu.SemaphoreType.DMA((groups, rows)),
        ] + scratch
    pieces = pl.pallas_call(
        functools.partial(solve_kernel, rim is not None, chan_size, 2.0 / off),
        out_shape=jax.ShapeDtypeStruct(piece, jnp.float32),
        in_specs=[pl.BlockSpec(memory_space=pltpu.SMEM), vmem, vmem]
        + ([anywhere] if rim is None else [vmem, vmem]),
        out_specs=anywhere,
        scratch_shapes=scratch,
        compiler_params=pltpu.CompilerParams(
            vmem_limit_bytes=first_vmem_bytes if rim is None else vmem_bytes
        ),
        cost_estimate=pl.CostEstimate(
            flops=200 * source.size, bytes_accessed=16 * source.size, transcendentals=0
        ),
        name="solve_rim" if rim is not None else "solve_inner",
    )(*operands)
    if not aligned:
        pieces = jnp.transpose(pieces.reshape(count, nchan, parts, block), (2, 0, 1, 3))
    return pieces


def mats_kernel(coupling_ref, column_ref, row_ref, out_ref):
    raw = coupling_ref[0]
    total = raw.shape[0]
    same = column_ref[...] == row_ref[...]
    mat = jnp.where(same, 0.5 * (raw + raw.T), 0.0)
    high = mat.astype(jnp.bfloat16)
    low = (mat - high.astype(jnp.float32)).astype(jnp.bfloat16)
    out_ref[0, :, 0:total] = high
    out_ref[0, :, total:2 * total] = high
    out_ref[0, :, 2 * total:3 * total] = low


def split_mats(coupling, channels):
    orders, total, _ = coupling.shape
    group = channels[:, 2]
    return pl.pallas_call(
        mats_kernel,
        grid=(orders,),
        out_shape=jax.ShapeDtypeStruct((orders, total, 3 * total), jnp.bfloat16),
        in_specs=[
            pl.BlockSpec((1, total, total), lambda k: (k, 0, 0)),
            pl.BlockSpec((total, 1), lambda k: (0, 0)),
            pl.BlockSpec((1, total), lambda k: (0, 0)),
        ],
        out_specs=pl.BlockSpec((1, total, 3 * total), lambda k: (k, 0, 0)),
        compiler_params=pltpu.CompilerParams(vmem_limit_bytes=vmem_bytes),
        cost_estimate=pl.CostEstimate(
            flops=4 * coupling.size, bytes_accessed=10 * coupling.size, transcendentals=0
        ),
        name="split_mats",
    )(coupling, group[:, None], group[None, :])


def repel_kernel(points_ref, mats_ref, factors_ref, out_ref, field_ref, parts_ref):
    orders, total, _ = mats_ref.shape
    groups, count, nchan, block = points_ref.shape
    chunk = min(256, total)

    def put(slot, start, value):
        high = value.astype(jnp.bfloat16)
        low = (value - high.astype(jnp.float32)).astype(jnp.bfloat16)
        size = value.shape[0]
        parts_ref[slot, start:start + size] = high
        parts_ref[slot, total + start:total + start + size] = low
        parts_ref[slot, 2 * total + start:2 * total + start + size] = high

    weights = (-step_tau, step_tau * step_tau / 2.0, -step_tau * step_tau * step_tau / 6.0)
    for n in range(count):
        for group in range(groups):
            field_ref[group * nchan:(group + 1) * nchan] = points_ref[group, n]
        for start in range(0, total, chunk):
            put(0, start, field_ref[start:start + chunk])
        for stage, weight in enumerate(weights):
            slot = stage % 2
            for start in range(0, total, chunk):
                rows = slice(start, start + chunk)
                value = None
                for k in range(orders):
                    term = factors_ref[n, k:k + 1] * jnp.dot(
                        mats_ref[k, rows], parts_ref[slot], preferred_element_type=jnp.float32
                    )
                    value = term if value is None else value + term
                if stage < 2:
                    put(1 - slot, start, value)
                field_ref[rows] += weight * value
        for group in range(groups):
            out_ref[group, n] = field_ref[group * nchan:(group + 1) * nchan]


def repel(points, mats, factors):
    groups, count, nchan, block = points.shape
    orders, total, _ = mats.shape
    vmem = pl.BlockSpec(memory_space=pltpu.VMEM)
    return pl.pallas_call(
        repel_kernel,
        out_shape=jax.ShapeDtypeStruct(points.shape, jnp.float32),
        in_specs=[vmem] * 3,
        out_specs=vmem,
        scratch_shapes=[
            pltpu.VMEM((total, block), jnp.float32),
            pltpu.VMEM((2, 3 * total, block), jnp.bfloat16),
        ],
        compiler_params=pltpu.CompilerParams(vmem_limit_bytes=vmem_bytes),
        cost_estimate=pl.CostEstimate(
            flops=3 * orders * 3 * 2 * total * points.size,
            bytes_accessed=2 * mats.size + 8 * points.size,
            transcendentals=0,
        ),
        name="repel",
    )(points, mats, factors)


def gather_kernel(targets, piece_ref, *refs):
    sems = refs[-1]
    out_ref = refs[-2]
    length = out_ref.shape[-1]
    copies = []
    for n, row in enumerate(targets):
        if piece_ref.ndim == 4:
            parts, _, _, block = piece_ref.shape
            for part in range(parts):
                columns = pl.ds(part * block, block)
                copies.append((piece_ref.at[part, n], out_ref.at[:, row, columns]))
        else:
            copies.append((piece_ref.at[n], out_ref.at[:, row, :]))
    copies = [pltpu.make_async_copy(*ends, sems.at[k]) for k, ends in enumerate(copies)]
    for copy in copies:
        copy.start()
    for copy in copies:
        copy.wait()


def gather_rows(piece, targets, earlier, shape):
    nchan, rows, length = shape
    parts, count, _, block = piece.shape
    if block % lanes or nchan % 8:
        piece = jnp.transpose(piece, (1, 2, 0, 3)).reshape(count, nchan, length)
    anywhere = pl.BlockSpec(memory_space=pl.ANY)
    operands = [piece] if earlier is None else [piece, earlier]
    return pl.pallas_call(
        functools.partial(gather_kernel, targets),
        out_shape=jax.ShapeDtypeStruct(shape, jnp.float32),
        in_specs=[anywhere] * len(operands),
        out_specs=anywhere,
        scratch_shapes=[pltpu.SemaphoreType.DMA((count * parts,))],
        input_output_aliases={} if earlier is None else {1: 0},
        compiler_params=pltpu.CompilerParams(vmem_limit_bytes=vmem_bytes),
        cost_estimate=pl.CostEstimate(
            flops=0, bytes_accessed=4 * count * nchan * length, transcendentals=0
        ),
        name="gather_first" if earlier is None else "gather_last",
    )(*operands)


def potential(lvalue, radius):
    return -2.0 / radius + lvalue * (lvalue + 1.0) / (2.0 * radius * radius)


def radial_factors(rfirst, rsecond):
    rmin = jnp.minimum(rsecond[:, None], rfirst[None, :])
    rmax = jnp.maximum(rsecond[:, None], rfirst[None, :])
    return jnp.stack(
        [1.0 / rmax, rmin / (rmax * rmax), rmin * rmin / (rmax * rmax * rmax)], axis=1
    )


def swap_halves(part, axis, devices):
    return lax.ppermute(part, axis, [(i, (i + devices // 2) % devices) for i in range(devices)])


def on_device(parts, rads, wave, coupling, channels):
    nchan, rows, length = wave.shape
    rad_index, chan_index = lax.axis_index("rad"), lax.axis_index("chan")
    numbers = channels.T
    inner = tuple(range(1, rows - 1))
    outer = (0, rows - 1)
    more = -nchan % 8
    padded = jnp.pad(wave, ((0, more), (0, 0), (0, 0))) if more else wave

    def exchange(pieces):
        return lax.all_to_all(pieces, "chan", 0, 0, tiled=True)

    first = solve_rows(len(inner), numbers, padded, None, parts, nchan)
    edge, partial = outer_rows(numbers, padded, nchan)
    rim = swap_halves(edge, "rad", rads)
    second = solve_rows(len(outer), numbers, partial, rim, parts, nchan)
    if more:
        first, second = first[:, :, :nchan], second[:, :, :nchan]

    block = length // parts
    rsecond = (rad_index * rows + jnp.arange(rows) + 1).astype(jnp.float32) * step_h + row_start
    points = (chan_index * block + jnp.arange(block) + 1).astype(jnp.float32) * (box_first / length)
    factors = radial_factors(points, rsecond)
    mats = split_mats(coupling, channels)
    result = None
    for here, pieces in ((inner, first), (outer, second)):
        chosen = jnp.stack([factors[r] for r in here])
        pieces = exchange(repel(exchange(pieces), mats, chosen))
        result = gather_rows(pieces, here, result, wave.shape)
    return result


def solution(mesh):
    in_specs = (P("chan", "rad", None), P(), P())
    out_specs = P("chan", "rad", None)
    return jax.shard_map(
        functools.partial(on_device, mesh.shape["chan"], mesh.shape["rad"]),
        mesh=mesh,
        in_specs=in_specs,
        out_specs=out_specs,
        check_vma=False,
    )
```
